256 devices in a mesh: dp: 32 (over x, y, core), mp: 8 (over z).
Axes of the slice: x: 4, y: 4, z: 8, core: 2. Of those that a mesh axis runs over, the one named last changes fastest.
Arguments:
- grads: bfloat16 [128, 1024, 1024], P(None, 'dp', 'mp')
- order: int32 [128], replicated, may hold values from 0 to 127, each once
- left_stat: float32 [256, 512, 1024], P(('dp', 'mp'))
- right_stat: float32 [256, 512, 1024], P(('dp', 'mp'))
- left_root: bfloat16 [256, 512, 1024], P(('dp', 'mp'))
- right_root: bfloat16 [256, 512, 1024], P(('dp', 'mp'))
Outputs:
- new_left: float32 [256, 512, 1024], P(('dp', 'mp'))
- new_right: float32 [256, 512, 1024], P(('dp', 'mp'))
- update: bfloat16 [128, 1024, 1024], P(None, 'dp', 'mp')
The draws below stay inside these ranges and needn't reach their ends.
Inputs may be any that keep to these rules, and one draw needn't show every extreme that they name: `order`: each block number appears exactly once.
All inputs are finite; a program needn't handle non-finite values.
Results may differ from the reference program's by a relative error of at most 0.0049.
Values may be sent and summed in bfloat16 or wider, within the bound.
A program may use at most 64 MiB of HBM per device.

```python
import jax
import jax.numpy as jnp
from jax import lax

BS = 1024
NBLK = 128


def symmetric(key, scale, diag):
    raw = jax.random.normal(key, (NBLK, BS, BS), jnp.float32)
    sym = 0.5 * (raw + jnp.swapaxes(raw, 1, 2)) * scale + diag * jnp.eye(BS, dtype=jnp.float32)
    return sym.reshape(2 * NBLK, BS // 2, BS)


def draw_grads(key, part):
    key = jax.random.fold_in(key, 1)
    key_a, key_b, key_c = jax.random.split(key, 3)
    ramp = jnp.arange(BS, dtype=jnp.float32) / (BS - 1)
    base = jax.random.normal(key_a, (NBLK, BS, BS), jnp.float32)
    spread = jnp.log(10.0)
    row_scale = jnp.exp(jax.random.uniform(key_b, (NBLK, BS, 1), jnp.float32) * spread) * jnp.power(3.0, ramp)[None, :, None]
    col_scale = jnp.exp(jax.random.uniform(key_c, (NBLK, 1, BS), jnp.float32) * spread) * jnp.power(3.0, ramp)[None, None, :]
    return (base * row_scale * col_scale).astype(jnp.bfloat16)


def draw_left_stat(key, part):
    key = jax.random.fold_in(key, 2)
    return symmetric(key, 1.0, 4.0)


def draw_right_stat(key, part):
    key = jax.random.fold_in(key, 3)
    return symmetric(key, 1.0, 4.0)


def draw_left_root(key, part):
    key = jax.random.fold_in(key, 4)
    return symmetric(key, BS ** (-0.5), 1.0).astype(jnp.bfloat16)


def draw_right_root(key, part):
    key = jax.random.fold_in(key, 5)
    return symmetric(key, BS ** (-0.5), 1.0).astype(jnp.bfloat16)


def setup_inputs(seed: int = 0) -> dict:
    seeds = jax.random.split(jax.random.key(seed), 7)
    return {
        "grads": draw_grads(jax.random.fold_in(seeds[6], 71), 0),
        "order": jax.random.permutation(seeds[1], NBLK).astype(jnp.int32),
        "left_stat": draw_left_stat(jax.random.fold_in(seeds[6], 71), 0),
        "right_stat": draw_right_stat(jax.random.fold_in(seeds[6], 71), 0),
        "left_root": draw_left_root(jax.random.fold_in(seeds[6], 71), 0),
        "right_root": draw_right_root(jax.random.fold_in(seeds[6], 71), 0),
    }


beta_two = 0.95
clip_rms = 0.5

def reference(grads, order, left_stat, right_stat, left_root, right_root):
    blocks = grads.shape[0]
    width = grads.shape[1]
    full_left = left_stat.reshape(blocks, width, width)
    full_right = right_stat.reshape(blocks, width, width)
    root_left = left_root.reshape(blocks, width, width)
    root_right = right_root.reshape(blocks, width, width)
    floats = grads.astype(jnp.float32)
    total = jnp.sum(floats * floats)
    clip = jnp.minimum(1.0, clip_rms * jnp.sqrt(jnp.float32(blocks * width * width)) / jnp.sqrt(total + 1e-06))
    high = lax.Precision.HIGHEST

    def one_slot(slot):
        block = order[slot]
        grad = lax.dynamic_index_in_dim(grads, block, 0, False).astype(jnp.float32)
        gram_left = jnp.dot(grad, grad.T, precision=high)
        gram_right = jnp.dot(grad.T, grad, precision=high)
        new_l = beta_two * full_left[slot] + (1.0 - beta_two) * clip * clip * gram_left
        new_r = beta_two * full_right[slot] + (1.0 - beta_two) * clip * clip * gram_right
        product = jnp.dot(root_left[slot].astype(jnp.float32), grad, precision=high).astype(jnp.bfloat16)
        product = lax.optimization_barrier(product).astype(jnp.float32)
        precond = jnp.dot(product, root_right[slot].astype(jnp.float32), precision=high)
        grad_sq = jnp.sum(grad * grad)
        upd_sq = jnp.sum(precond * precond)
        graft = clip * jnp.sqrt(grad_sq) / jnp.sqrt(upd_sq + 1e-06)
        return (new_l, new_r, (-graft * precond).astype(jnp.bfloat16))
    new_l, new_r, slot_upd = lax.map(one_slot, jnp.arange(blocks, dtype=jnp.int32))
    update = jnp.zeros_like(slot_upd).at[order].set(slot_upd)
    return (new_l.reshape(left_stat.shape), new_r.reshape(right_stat.shape), update)
```

```python
import functools

import jax
import jax.numpy as jnp
from jax import lax
from jax.experimental import pallas as pl
from jax.experimental.pallas import tpu as pltpu
from jax.sharding import PartitionSpec as P

MESH = pl.DeviceIdType.MESH
F32 = jnp.float32
BF16 = jnp.bfloat16
beta_two = 0.95
clip_rms = 0.5


def fold(x):
    x = x.astype(F32)
    return jnp.sum((x * x).reshape(-1, 8, 128), axis=0)


def everything(x):
    return jnp.sum(jnp.sum(x, axis=0, keepdims=True), axis=1, keepdims=True)


def kernel(
    nd,
    nm,
    order_in,
    grads_in,
    left_stat,
    right_stat,
    left_root,
    right_root,
    new_left,
    new_right,
    u_in,
    scales,
    order,
    grads,
    tiles,
    slabs,
    full,
    lroot,
    rroot,
    acc,
    last_a,
    u_out,
    sq_dp,
    sq_mine,
    sq_mp,
    g_sq,
    sums,
    load_sem,
    slab_sem,
    tile_sem,
    forward_sem,
    root_sem,
    sq_send_sem,
    sq_recv_sem,
    sum_send_sem,
    sum_recv_sem,
    u_send_sem,
    u_recv_sem,
    ready_sem,
):
    blocks, rows, cols = grads.shape
    half, width = lroot.shape
    pairs = nm // 2
    d = lax.axis_index("dp")
    m = lax.axis_index("mp")
    h = m % 2
    pair = m // 2
    sigma = 2 * h - 1
    partner = m - sigma
    per_half = nd // 2
    my_rows = pl.ds(pl.multiple_of(h * half, half), half)

    def place(offset):
        return (m + offset + 2 * nm) % nm

    first_loads = [
        pltpu.make_async_copy(order_in.at[0], order, load_sem.at[4]),
        pltpu.make_async_copy(grads_in, grads, load_sem.at[5]),
    ]
    for load in first_loads:
        load.start()

    barrier = pltpu.get_barrier_semaphore()

    def greet(k, carry):
        pl.semaphore_signal(barrier, inc=1, device_id=((d + k) % nd, m), device_id_type=MESH)
        return carry

    lax.fori_loop(1, nd, greet, 0)
    for k in range(1, nm):
        pl.semaphore_signal(barrier, inc=1, device_id=(d, (m + k) % nm), device_id_type=MESH)

    loads = [
        pltpu.make_async_copy(left_root.at[0], lroot, load_sem.at[0]),
        pltpu.make_async_copy(right_root.at[0], rroot.at[my_rows], load_sem.at[1]),
        pltpu.make_async_copy(left_stat, new_left, load_sem.at[2]),
        pltpu.make_async_copy(right_stat, new_right, load_sem.at[3]),
    ]

    pl.semaphore_wait(barrier, nd - 1 + nm - 1)
    for k in range(1, nm):
        pl.semaphore_signal(ready_sem, inc=1, device_id=(d, (m + k) % nm), device_id_type=MESH)

    part_rows = half // 4

    def root_copy(n):
        return pltpu.make_async_remote_copy(
            src_ref=right_root.at[0, pl.ds(n * part_rows, part_rows)],
            dst_ref=rroot.at[pl.ds(pl.multiple_of(h * half + n * part_rows, part_rows), part_rows)],
            send_sem=root_sem.at[0],
            recv_sem=root_sem.at[1],
            device_id=(d, partner),
            device_id_type=MESH,
        )

    root_copy(0).start()
    for load in loads:
        load.start()

    targets = [place(3 * sigma), place(-2 * sigma), place(sigma), m]

    def tile_copy(there, target):
        return pltpu.make_async_remote_copy(
            src_ref=tiles.at[pairs * there + target // 2],
            dst_ref=slabs.at[m, pl.ds(pl.multiple_of(d * rows, rows), rows)],
            send_sem=tile_sem,
            recv_sem=slab_sem.at[m],
            device_id=(there, target),
            device_id_type=MESH,
        )

    def arrange(there, total):
        for p in range(pairs):
            s = pairs * there + p
            tile = grads[order[s]]
            tiles[s] = tile
            total = total + fold(tile)
        return total

    for load in first_loads:
        load.wait()
    pl.semaphore_wait(ready_sem, nm - 1)
    total = arrange(d, jnp.zeros((8, 128), F32))
    for target in targets[:3]:
        tile_copy(d, target).start()
    pltpu.make_async_copy(
        tiles.at[pairs * d + pair],
        slabs.at[m, pl.ds(pl.multiple_of(d * rows, rows), rows)],
        slab_sem.at[m],
    ).start()

    def send_tiles(k, total):
        there = (d + k) % nd
        total = arrange(there, total)
        for target in targets:
            tile_copy(there, target).start()
        return total

    sq_dp[d] = lax.fori_loop(1, nd, send_tiles, total)

    for n in range(1, 4):
        root_copy(n).start()

    def send_sq(k, carry):
        pltpu.make_async_remote_copy(
            src_ref=sq_dp.at[d],
            dst_ref=sq_dp.at[d],
            send_sem=sq_send_sem.at[0],
            recv_sem=sq_recv_sem.at[0],
            device_id=((d + k) % nd, m),
            device_id_type=MESH,
        ).start()
        return carry

    lax.fori_loop(1, nd, send_sq, 0)
    some = sq_dp.at[pl.ds(0, nd - 1)]
    pltpu.make_async_copy(some, some, sq_recv_sem.at[0]).wait()
    sq_mine[...] = jnp.sum(sq_dp[...], axis=0)
    sq_mp[m] = sq_mine[...]
    for k in range(1, nm):
        pltpu.make_async_remote_copy(
            src_ref=sq_mine,
            dst_ref=sq_mp.at[m],
            send_sem=sq_send_sem.at[1],
            recv_sem=sq_recv_sem.at[1],
            device_id=(d, (m + k) % nm),
            device_id_type=MESH,
        ).start()

    def wait_slab(k):
        pltpu.make_async_copy(slabs.at[k], slabs.at[k], slab_sem.at[k]).wait()

    def forward(k):
        return pltpu.make_async_remote_copy(
            src_ref=slabs.at[k],
            dst_ref=slabs.at[k],
            send_sem=forward_sem.at[k],
            recv_sem=slab_sem.at[k],
            device_id=(d, partner),
            device_id_type=MESH,
        )

    for j in range(pairs):
        k = place(j * sigma)
        wait_slab(k)
        forward(k).start()

    loads[0].wait()
    loads[1].wait()
    pltpu.make_async_copy(lroot, lroot, root_sem.at[1]).wait()
    acc[...] = jnp.zeros_like(acc)
    g_sq[...] = jnp.zeros_like(g_sq)

    def through_left(k):
        slab = slabs[k]
        g_sq[...] += fold(slab)
        return jnp.dot(lroot[...], slab, preferred_element_type=F32).astype(BF16)

    def right_rows(k):
        return pl.ds(pl.multiple_of(k * cols, cols), cols)

    def use_slab(k):
        a = through_left(k)
        acc[...] += jnp.dot(a, rroot[right_rows(k)], preferred_element_type=F32)

    def near(j, carry):
        use_slab(place(j * sigma))
        return carry

    def far(j, carry):
        k = place(-(j + 1) * sigma)
        wait_slab(k)
        use_slab(k)
        return carry

    lax.fori_loop(0, pairs, near, 0)
    lax.fori_loop(0, pairs - 1, far, 0)
    last = place(-pairs * sigma)
    wait_slab(last)
    last_a[...] = through_left(last)
    step = 2 * cols

    def finish(n, total):
        part = pl.ds(pl.multiple_of(n * step, step), step)
        u = acc[:, part] + jnp.dot(
            last_a[...], rroot[right_rows(last), part], preferred_element_type=F32
        )
        u_out[2 * n] = u[:, :cols].astype(BF16)
        u_out[2 * n + 1] = u[:, cols:].astype(BF16)
        return total + fold(u[:, :cols]) + fold(u[:, cols:])

    u_sq = lax.fori_loop(0, pairs, finish, jnp.zeros((8, 128), F32))

    row = lax.broadcasted_iota(jnp.int32, (8, 128), 0)
    sums[m] = jnp.where(row < 4, everything(u_sq), everything(g_sq[...]))
    for k in range(1, nm):
        pltpu.make_async_remote_copy(
            src_ref=sums.at[m],
            dst_ref=sums.at[m],
            send_sem=sum_send_sem.at[0],
            recv_sem=sum_recv_sem.at[0],
            device_id=(d, (m + k) % nm),
            device_id_type=MESH,
        ).start()

    slot = pairs * d + pair

    def u_copy(near_row, target):
        return pltpu.make_async_remote_copy(
            src_ref=u_out.at[target, pl.ds(pl.multiple_of(near_row * rows, rows), rows)],
            dst_ref=u_in.at[slot],
            send_sem=u_send_sem,
            recv_sem=u_recv_sem,
            device_id=(h * per_half + near_row, target),
            device_id_type=MESH,
        )

    own_half = d // per_half == h

    def send_u(k, carry):
        near_row = (d + k) % per_half
        for j in range(1, nm):
            u_copy(near_row, (m + j) % nm).start()
        here = jnp.logical_and(own_half, k == 0)

        @pl.when(here)
        def _():
            pltpu.make_async_copy(
                u_out.at[m, pl.ds(pl.multiple_of(near_row * rows, rows), rows)],
                u_in.at[slot],
                u_recv_sem,
            ).start()

        @pl.when(jnp.logical_not(here))
        def _():
            u_copy(near_row, m).start()

        return carry

    lax.fori_loop(0, per_half // 2, send_u, 0)

    some_mp = sq_mp.at[pl.ds(0, nm - 1)]
    pltpu.make_async_copy(some_mp, some_mp, sq_recv_sem.at[1]).wait()
    total_sq = everything(jnp.sum(sq_mp[...], axis=0))
    clip = jnp.minimum(1.0, clip_rms * jnp.sqrt(F32(blocks * width * width)) / jnp.sqrt(total_sq + 1e-06))
    coefficient = (1.0 - beta_two) * clip * clip
    pltpu.make_async_copy(some_mp, some_mp, sum_recv_sem.at[0]).wait()
    mine = jnp.zeros((8, 128), F32)
    for p in range(pairs):
        u_total = sums[2 * p, 0:1] + sums[2 * p + 1, 0:1]
        scale = -(clip * jnp.sqrt(sums[2 * p, 4:5]) / jnp.sqrt(u_total + 1e-06))
        mine = jnp.where(row == p, scale, mine)
    scales[d] = mine

    def send_scales(k, carry):
        pltpu.make_async_remote_copy(
            src_ref=scales.at[d],
            dst_ref=scales.at[d],
            send_sem=sum_send_sem.at[1],
            recv_sem=sum_recv_sem.at[1],
            device_id=((d + k) % nd, m),
            device_id_type=MESH,
        ).start()
        return carry

    lax.fori_loop(1, nd, send_scales, 0)
    lax.fori_loop(per_half // 2, per_half, send_u, 0)

    for k in range(nm):
        full[:, k * cols : (k + 1) * cols] = slabs[k]
    loads[2].wait()

    def left_gram(n, carry):
        part = pl.ds(pl.multiple_of(n * step, step), step)
        gram = lax.dot_general(
            full[my_rows], full[part], (((1,), (1,)), ((), ())), preferred_element_type=F32
        )
        new_left[0, :, part] = beta_two * new_left[0, :, part] + coefficient * gram
        return carry

    lax.fori_loop(0, width // step, left_gram, 0)
    loads[3].wait()

    def right_gram(n, carry):
        part = pl.ds(pl.multiple_of(n * step, step), step)
        gram = lax.dot_general(
            full[:, my_rows], full[:, part], (((0,), (0,)), ((), ())), preferred_element_type=F32
        )
        new_right[0, :, part] = beta_two * new_right[0, :, part] + coefficient * gram
        return carry

    lax.fori_loop(0, width // step, right_gram, 0)

    sent = tiles.at[pl.ds(0, blocks - 1)]
    pltpu.make_async_copy(sent, sent, tile_sem).wait()
    pltpu.make_async_copy(lroot, lroot, root_sem.at[0]).wait()
    pltpu.make_async_copy(some, some, sq_send_sem.at[0]).wait()
    pltpu.make_async_copy(some_mp, some_mp, sq_send_sem.at[1]).wait()
    pltpu.make_async_copy(some_mp, some_mp, sum_send_sem.at[0]).wait()
    pltpu.make_async_copy(some, some, sum_send_sem.at[1]).wait()
    for j in range(pairs):
        forward(place(j * sigma)).wait_send()

    @pl.when(own_half)
    def _():
        pltpu.make_async_copy(sent, sent, u_send_sem).wait()

    @pl.when(jnp.logical_not(own_half))
    def _():
        pltpu.make_async_copy(tiles, tiles, u_send_sem).wait()

    pltpu.make_async_copy(some, some, sum_recv_sem.at[1]).wait()
    pltpu.make_async_copy(u_in, u_in, u_recv_sem).wait()


def finish_kernel(order_in, left, right, tiles, scales, new_left, new_right, update, order, arranged, sem):
    blocks = tiles.shape[0]
    pairs = blocks // scales.shape[0]
    order_copy = pltpu.make_async_copy(order_in.at[0], order, sem.at[0])
    order_copy.start()
    stores = [
        pltpu.make_async_copy(left, new_left, sem.at[1]),
        pltpu.make_async_copy(right, new_right, sem.at[2]),
    ]
    for store in stores:
        store.start()
    order_copy.wait()

    def give(there, carry):
        for p in range(pairs):
            s = pairs * there + p
            arranged[order[s]] = (tiles[s].astype(F32) * scales[there, p : p + 1]).astype(BF16)
        return carry

    lax.fori_loop(0, scales.shape[0], give, 0, unroll=2)
    last = pltpu.make_async_copy(arranged, update, sem.at[3])
    last.start()
    last.wait()
    for store in stores:
        store.wait()


def body(nd, nm, grads, order, left_stat, right_stat, left_root, right_root):
    blocks, rows, cols = grads.shape
    _, half, width = left_stat.shape
    vmem = pl.BlockSpec(memory_space=pltpu.VMEM)
    half_shape = left_stat.shape
    hbm = pl.BlockSpec(memory_space=pltpu.HBM)
    dma = pltpu.SemaphoreType.DMA
    operands = [order.reshape(1, blocks), grads, left_stat, right_stat, left_root, right_root]
    operands = [pltpu.with_memory_space_constraint(x, pltpu.HBM) for x in operands]
    products = 4 * half * width * width
    results = pl.pallas_call(
        functools.partial(kernel, nd, nm),
        out_shape=(
            pltpu.VMEM(left_stat.shape, F32),
            pltpu.VMEM(right_stat.shape, F32),
            pltpu.VMEM(grads.shape, BF16),
            pltpu.VMEM((nd, 8, 128), F32),
        ),
        in_specs=[hbm] * 6,
        out_specs=(vmem, vmem, vmem, vmem),
        scratch_shapes=[
            pltpu.SMEM((blocks,), jnp.int32),
            pltpu.VMEM((blocks, rows, cols), BF16),
            pltpu.VMEM((blocks, rows, cols), BF16),
            pltpu.VMEM((nm, width, cols), BF16),
            pltpu.VMEM((width, width), BF16),
            pltpu.VMEM((half, width), BF16),
            pltpu.VMEM((width, width), BF16),
            pltpu.VMEM((half, width), F32),
            pltpu.VMEM((half, cols), BF16),
            pltpu.VMEM((nm, half, cols), BF16),
            pltpu.VMEM((nd, 8, 128), F32),
            pltpu.VMEM((8, 128), F32),
            pltpu.VMEM((nm, 8, 128), F32),
            pltpu.VMEM((8, 128), F32),
            pltpu.VMEM((nm, 8, 128), F32),
            dma((6,)),
            dma((nm,)),
            dma,
            dma((nm,)),
            dma((2,)),
            dma((2,)),
            dma((2,)),
            dma((2,)),
            dma((2,)),
            dma,
            dma,
            pltpu.SemaphoreType.REGULAR,
        ],
        compiler_params=pltpu.CompilerParams(
            collective_id=0, has_side_effects=True, vmem_limit_bytes=48 * 1024 * 1024
        ),
        cost_estimate=pl.CostEstimate(
            flops=2 * products, bytes_accessed=12 * half * width * 2, transcendentals=0
        ),
        name="step",
    )(*operands)
    return pl.pallas_call(
        finish_kernel,
        out_shape=(
            pltpu.HBM(half_shape, F32),
            pltpu.HBM(half_shape, F32),
            pltpu.HBM(grads.shape, BF16),
        ),
        in_specs=[hbm, vmem, vmem, vmem, vmem],
        out_specs=(hbm, hbm, hbm),
        scratch_shapes=[
            pltpu.SMEM((blocks,), jnp.int32),
            pltpu.VMEM(grads.shape, BF16),
            dma((4,)),
        ],
        compiler_params=pltpu.CompilerParams(vmem_limit_bytes=8 * 1024 * 1024),
        cost_estimate=pl.CostEstimate(flops=0, bytes_accessed=10 * half * width, transcendentals=0),
        name="finish",
    )(operands[0], *results)


def solution(mesh):
    owned = P(("dp", "mp"), None, None)
    return jax.shard_map(
        functools.partial(body, mesh.shape["dp"], mesh.shape["mp"]),
        mesh=mesh,
        in_specs=(P(None, "dp", "mp"), P(), owned, owned, owned, owned),
        out_specs=(owned, owned, P(None, "dp", "mp")),
        check_vma=False,
    )
```

```python
import functools

import jax
import jax.numpy as jnp
from jax import lax
from jax.experimental import pallas as pl
from jax.experimental.pallas import tpu as pltpu
from jax.sharding import PartitionSpec as P

MESH = pl.DeviceIdType.MESH
F32 = jnp.float32
BF16 = jnp.bfloat16
beta_two = 0.95
clip_rms = 0.5


def fold(x):
    x = x.astype(F32)
    return jnp.sum((x * x).reshape(-1, 8, 128), axis=0)


def everything(x):
    return jnp.sum(jnp.sum(x, axis=0, keepdims=True), axis=1, keepdims=True)


def kernel(
    nd,
    nm,
    order_in,
    grads_in,
    left_stat,
    right_stat,
    left_root,
    right_root,
    new_left,
    new_right,
    u_in,
    scales,
    order,
    grads,
    tiles,
    slabs,
    full,
    lroot,
    rroot,
    acc,
    last_a,
    u_out,
    relay,
    sq_dp,
    sq_mine,
    sq_mp,
    g_sq,
    sums,
    load_sem,
    slab_sem,
    tile_sem,
    forward_sem,
    root_sem,
    sq_send_sem,
    sq_recv_sem,
    sum_send_sem,
    sum_recv_sem,
    u_send_sem,
    u_recv_sem,
    relay_sem,
    ready_sem,
):
    blocks, rows, cols = grads.shape
    half, width = lroot.shape
    pairs = nm // 2
    d = lax.axis_index("dp")
    m = lax.axis_index("mp")
    h = m % 2
    pair = m // 2
    sigma = 2 * h - 1
    partner = m - sigma
    per_half = nd // 2
    my_rows = pl.ds(pl.multiple_of(h * half, half), half)

    def place(offset):
        return (m + offset + 2 * nm) % nm

    first_loads = [
        pltpu.make_async_copy(order_in.at[0], order, load_sem.at[4]),
        pltpu.make_async_copy(grads_in, grads, load_sem.at[5]),
    ]
    for load in first_loads:
        load.start()

    barrier = pltpu.get_barrier_semaphore()

    def greet(k, carry):
        pl.semaphore_signal(barrier, inc=1, device_id=((d + k) % nd, m), device_id_type=MESH)
        return carry

    lax.fori_loop(1, nd, greet, 0)
    for k in range(1, nm):
        pl.semaphore_signal(barrier, inc=1, device_id=(d, (m + k) % nm), device_id_type=MESH)

    loads = [
        pltpu.make_async_copy(left_root.at[0], lroot, load_sem.at[0]),
        pltpu.make_async_copy(right_root.at[0], rroot.at[my_rows], load_sem.at[1]),
        pltpu.make_async_copy(left_stat, new_left, load_sem.at[2]),
        pltpu.make_async_copy(right_stat, new_right, load_sem.at[3]),
    ]

    pl.semaphore_wait(barrier, nd - 1 + nm - 1)
    for k in range(1, nm):
        pl.semaphore_signal(ready_sem, inc=1, device_id=(d, (m + k) % nm), device_id_type=MESH)

    part_rows = half // 4

    def root_copy(n):
        return pltpu.make_async_remote_copy(
            src_ref=right_root.at[0, pl.ds(n * part_rows, part_rows)],
            dst_ref=rroot.at[pl.ds(pl.multiple_of(h * half + n * part_rows, part_rows), part_rows)],
            send_sem=root_sem.at[0],
            recv_sem=root_sem.at[1],
            device_id=(d, partner),
            device_id_type=MESH,
        )

    root_copy(0).start()
    for load in loads:
        load.start()

    targets = [place(3 * sigma), place(-2 * sigma), place(sigma), m]

    def tile_copy(there, target):
        return pltpu.make_async_remote_copy(
            src_ref=tiles.at[pairs * there + target // 2],
            dst_ref=slabs.at[m, pl.ds(pl.multiple_of(d * rows, rows), rows)],
            send_sem=tile_sem,
            recv_sem=slab_sem.at[m],
            device_id=(there, target),
            device_id_type=MESH,
        )

    def arrange(there, total):
        for p in range(pairs):
            s = pairs * there + p
            tile = grads[order[s]]
            tiles[s] = tile
            total = total + fold(tile)
        return total

    for load in first_loads:
        load.wait()
    pl.semaphore_wait(ready_sem, nm - 1)
    total = arrange(d, jnp.zeros((8, 128), F32))
    for target in targets[:3]:
        tile_copy(d, target).start()
    pltpu.make_async_copy(
        tiles.at[pairs * d + pair],
        slabs.at[m, pl.ds(pl.multiple_of(d * rows, rows), rows)],
        slab_sem.at[m],
    ).start()

    def send_tiles(k, total):
        there = (d + k) % nd
        total = arrange(there, total)
        for target in targets:
            tile_copy(there, target).start()
        return total

    sq_dp[d] = lax.fori_loop(1, nd, send_tiles, total)

    for n in range(1, 4):
        root_copy(n).start()

    def send_sq(k, carry):
        pltpu.make_async_remote_copy(
            src_ref=sq_dp.at[d],
            dst_ref=sq_dp.at[d],
            send_sem=sq_send_sem.at[0],
            recv_sem=sq_recv_sem.at[0],
            device_id=((d + k) % nd, m),
            device_id_type=MESH,
        ).start()
        return carry

    lax.fori_loop(1, nd, send_sq, 0)
    some = sq_dp.at[pl.ds(0, nd - 1)]
    pltpu.make_async_copy(some, some, sq_recv_sem.at[0]).wait()
    sq_mine[...] = jnp.sum(sq_dp[...], axis=0)
    sq_mp[m] = sq_mine[...]
    for k in range(1, nm):
        pltpu.make_async_remote_copy(
            src_ref=sq_mine,
            dst_ref=sq_mp.at[m],
            send_sem=sq_send_sem.at[1],
            recv_sem=sq_recv_sem.at[1],
            device_id=(d, (m + k) % nm),
            device_id_type=MESH,
        ).start()

    def wait_slab(k):
        pltpu.make_async_copy(slabs.at[k], slabs.at[k], slab_sem.at[k]).wait()

    def forward(k):
        return pltpu.make_async_remote_copy(
            src_ref=slabs.at[k],
            dst_ref=slabs.at[k],
            send_sem=forward_sem.at[k],
            recv_sem=slab_sem.at[k],
            device_id=(d, partner),
            device_id_type=MESH,
        )

    for j in range(pairs):
        k = place(j * sigma)
        wait_slab(k)
        forward(k).start()

    loads[0].wait()
    loads[1].wait()
    pltpu.make_async_copy(lroot, lroot, root_sem.at[1]).wait()
    acc[...] = jnp.zeros_like(acc)
    g_sq[...] = jnp.zeros_like(g_sq)

    def through_left(k):
        slab = slabs[k]
        g_sq[...] += fold(slab)
        return jnp.dot(lroot[...], slab, preferred_element_type=F32).astype(BF16)

    def right_rows(k):
        return pl.ds(pl.multiple_of(k * cols, cols), cols)

    def use_slab(k):
        a = through_left(k)
        acc[...] += jnp.dot(a, rroot[right_rows(k)], preferred_element_type=F32)

    def near(j, carry):
        use_slab(place(j * sigma))
        return carry

    def far(j, carry):
        k = place(-(j + 1) * sigma)
        wait_slab(k)
        use_slab(k)
        return carry

    lax.fori_loop(0, pairs, near, 0)
    lax.fori_loop(0, pairs - 1, far, 0)
    last = place(-pairs * sigma)
    wait_slab(last)
    last_a[...] = through_left(last)
    step = 2 * cols

    opposite = place(nm // 2)

    def finish(i, total):
        n = (opposite // 2 + i) % pairs
        part = pl.ds(pl.multiple_of(n * step, step), step)
        u = acc[:, part] + jnp.dot(
            last_a[...], rroot[right_rows(last), part], preferred_element_type=F32
        )
        u_out[2 * n] = u[:, :cols].astype(BF16)
        u_out[2 * n + 1] = u[:, cols:].astype(BF16)
        return total + fold(u[:, :cols]) + fold(u[:, cols:])

    u_sq = finish(0, jnp.zeros((8, 128), F32))
    relay_copy = pltpu.make_async_remote_copy(
        src_ref=u_out.at[opposite],
        dst_ref=relay,
        send_sem=relay_sem.at[0],
        recv_sem=relay_sem.at[1],
        device_id=(d, partner),
        device_id_type=MESH,
    )
    relay_copy.start()
    u_sq = lax.fori_loop(1, pairs, finish, u_sq)

    row = lax.broadcasted_iota(jnp.int32, (8, 128), 0)
    sums[m] = jnp.where(row < 4, everything(u_sq), everything(g_sq[...]))
    for k in range(1, nm):
        pltpu.make_async_remote_copy(
            src_ref=sums.at[m],
            dst_ref=sums.at[m],
            send_sem=sum_send_sem.at[0],
            recv_sem=sum_recv_sem.at[0],
            device_id=(d, (m + k) % nm),
            device_id_type=MESH,
        ).start()

    slot = pairs * d + pair

    def u_copy(near_row, target):
        return pltpu.make_async_remote_copy(
            src_ref=u_out.at[target, pl.ds(pl.multiple_of(near_row * rows, rows), rows)],
            dst_ref=u_in.at[slot],
            send_sem=u_send_sem,
            recv_sem=u_recv_sem,
            device_id=(h * per_half + near_row, target),
            device_id_type=MESH,
        )

    own_half = d // per_half == h

    def send_u(k, carry):
        near_row = (d + k) % per_half
        for j in range(1, nm):
            if j != nm // 2:
                u_copy(near_row, (m + j) % nm).start()
        here = jnp.logical_and(own_half, k == 0)

        @pl.when(here)
        def _():
            pltpu.make_async_copy(
                u_out.at[m, pl.ds(pl.multiple_of(near_row * rows, rows), rows)],
                u_in.at[slot],
                u_recv_sem,
            ).start()

        @pl.when(jnp.logical_not(here))
        def _():
            u_copy(near_row, m).start()

        return carry

    lax.fori_loop(0, per_half // 2, send_u, 0)
    relay_copy.wait_recv()

    def pass_on(k, carry):
        near_row = (d + k) % per_half
        pltpu.make_async_remote_copy(
            src_ref=relay.at[pl.ds(pl.multiple_of(near_row * rows, rows), rows)],
            dst_ref=u_in.at[slot],
            send_sem=u_send_sem,
            recv_sem=u_recv_sem,
            device_id=((1 - h) * per_half + near_row, (partner + nm // 2) % nm),
            device_id_type=MESH,
        ).start()
        return carry

    lax.fori_loop(0, per_half, pass_on, 0)

    some_mp = sq_mp.at[pl.ds(0, nm - 1)]
    pltpu.make_async_copy(some_mp, some_mp, sq_recv_sem.at[1]).wait()
    total_sq = everything(jnp.sum(sq_mp[...], axis=0))
    clip = jnp.minimum(1.0, clip_rms * jnp.sqrt(F32(blocks * width * width)) / jnp.sqrt(total_sq + 1e-06))
    coefficient = (1.0 - beta_two) * clip * clip
    pltpu.make_async_copy(some_mp, some_mp, sum_recv_sem.at[0]).wait()
    mine = jnp.zeros((8, 128), F32)
    for p in range(pairs):
        u_total = sums[2 * p, 0:1] + sums[2 * p + 1, 0:1]
        scale = -(clip * jnp.sqrt(sums[2 * p, 4:5]) / jnp.sqrt(u_total + 1e-06))
        mine = jnp.where(row == p, scale, mine)
    scales[d] = mine

    def send_scales(k, carry):
        pltpu.make_async_remote_copy(
            src_ref=scales.at[d],
            dst_ref=scales.at[d],
            send_sem=sum_send_sem.at[1],
            recv_sem=sum_recv_sem.at[1],
            device_id=((d + k) % nd, m),
            device_id_type=MESH,
        ).start()
        return carry

    lax.fori_loop(1, nd, send_scales, 0)
    lax.fori_loop(per_half // 2, per_half, send_u, 0)

    for k in range(nm):
        full[:, k * cols : (k + 1) * cols] = slabs[k]
    loads[2].wait()

    def left_gram(n, carry):
        part = pl.ds(pl.multiple_of(n * step, step), step)
        gram = lax.dot_general(
            full[my_rows], full[part], (((1,), (1,)), ((), ())), preferred_element_type=F32
        )
        new_left[0, :, part] = beta_two * new_left[0, :, part] + coefficient * gram
        return carry

    lax.fori_loop(0, width // step, left_gram, 0)
    loads[3].wait()

    def right_gram(n, carry):
        part = pl.ds(pl.multiple_of(n * step, step), step)
        gram = lax.dot_general(
            full[:, my_rows], full[:, part], (((0,), (0,)), ((), ())), preferred_element_type=F32
        )
        new_right[0, :, part] = beta_two * new_right[0, :, part] + coefficient * gram
        return carry

    lax.fori_loop(0, width // step, right_gram, 0)

    sent = tiles.at[pl.ds(0, blocks - 1)]
    pltpu.make_async_copy(sent, sent, tile_sem).wait()
    pltpu.make_async_copy(lroot, lroot, root_sem.at[0]).wait()
    pltpu.make_async_copy(some, some, sq_send_sem.at[0]).wait()
    pltpu.make_async_copy(some_mp, some_mp, sq_send_sem.at[1]).wait()
    pltpu.make_async_copy(some_mp, some_mp, sum_send_sem.at[0]).wait()
    pltpu.make_async_copy(some, some, sum_send_sem.at[1]).wait()
    relay_copy.wait_send()
    for j in range(pairs):
        forward(place(j * sigma)).wait_send()

    @pl.when(own_half)
    def _():
        pltpu.make_async_copy(sent, sent, u_send_sem).wait()

    @pl.when(jnp.logical_not(own_half))
    def _():
        pltpu.make_async_copy(tiles, tiles, u_send_sem).wait()

    pltpu.make_async_copy(some, some, sum_recv_sem.at[1]).wait()
    pltpu.make_async_copy(u_in, u_in, u_recv_sem).wait()


def finish_kernel(order_in, left, right, tiles, scales, new_left, new_right, update, order, arranged, sem):
    blocks = tiles.shape[0]
    pairs = blocks // scales.shape[0]
    order_copy = pltpu.make_async_copy(order_in.at[0], order, sem.at[0])
    order_copy.start()
    stores = [
        pltpu.make_async_copy(left, new_left, sem.at[1]),
        pltpu.make_async_copy(right, new_right, sem.at[2]),
    ]
    for store in stores:
        store.start()
    order_copy.wait()

    def give(there, carry):
        for p in range(pairs):
            s = pairs * there + p
            arranged[order[s]] = (tiles[s].astype(F32) * scales[there, p : p + 1]).astype(BF16)
        return carry

    lax.fori_loop(0, scales.shape[0], give, 0, unroll=2)
    last = pltpu.make_async_copy(arranged, update, sem.at[3])
    last.start()
    last.wait()
    for store in stores:
        store.wait()


def body(nd, nm, grads, order, left_stat, right_stat, left_root, right_root):
    blocks, rows, cols = grads.shape
    _, half, width = left_stat.shape
    vmem = pl.BlockSpec(memory_space=pltpu.VMEM)
    half_shape = left_stat.shape
    hbm = pl.BlockSpec(memory_space=pltpu.HBM)
    dma = pltpu.SemaphoreType.DMA
    operands = [order.reshape(1, blocks), grads, left_stat, right_stat, left_root, right_root]
    operands = [pltpu.with_memory_space_constraint(x, pltpu.HBM) for x in operands]
    products = 4 * half * width * width
    results = pl.pallas_call(
        functools.partial(kernel, nd, nm),
        out_shape=(
            pltpu.VMEM(left_stat.shape, F32),
            pltpu.VMEM(right_stat.shape, F32),
            pltpu.VMEM(grads.shape, BF16),
            pltpu.VMEM((nd, 8, 128), F32),
        ),
        in_specs=[hbm] * 6,
        out_specs=(vmem, vmem, vmem, vmem),
        scratch_shapes=[
            pltpu.SMEM((blocks,), jnp.int32),
            pltpu.VMEM((blocks, rows, cols), BF16),
            pltpu.VMEM((blocks, rows, cols), BF16),
            pltpu.VMEM((nm, width, cols), BF16),
            pltpu.VMEM((width, width), BF16),
            pltpu.VMEM((half, width), BF16),
            pltpu.VMEM((width, width), BF16),
            pltpu.VMEM((half, width), F32),
            pltpu.VMEM((half, cols), BF16),
            pltpu.VMEM((nm, half, cols), BF16),
            pltpu.VMEM((half, cols), BF16),
            pltpu.VMEM((nd, 8, 128), F32),
            pltpu.VMEM((8, 128), F32),
            pltpu.VMEM((nm, 8, 128), F32),
            pltpu.VMEM((8, 128), F32),
            pltpu.VMEM((nm, 8, 128), F32),
            dma((6,)),
            dma((nm,)),
            dma,
            dma((nm,)),
            dma((2,)),
            dma((2,)),
            dma((2,)),
            dma((2,)),
            dma((2,)),
            dma,
            dma,
            dma((2,)),
            pltpu.SemaphoreType.REGULAR,
        ],
        compiler_params=pltpu.CompilerParams(
            collective_id=0, has_side_effects=True, vmem_limit_bytes=48 * 1024 * 1024
        ),
        cost_estimate=pl.CostEstimate(
            flops=2 * products, bytes_accessed=12 * half * width * 2, transcendentals=0
        ),
        name="step",
    )(*operands)
    return pl.pallas_call(
        finish_kernel,
        out_shape=(
            pltpu.HBM(half_shape, F32),
            pltpu.HBM(half_shape, F32),
            pltpu.HBM(grads.shape, BF16),
        ),
        in_specs=[hbm, vmem, vmem, vmem, vmem],
        out_specs=(hbm, hbm, hbm),
        scratch_shapes=[
            pltpu.SMEM((blocks,), jnp.int32),
            pltpu.VMEM(grads.shape, BF16),
            dma((4,)),
        ],
        compiler_params=pltpu.CompilerParams(vmem_limit_bytes=8 * 1024 * 1024),
        cost_estimate=pl.CostEstimate(flops=0, bytes_accessed=10 * half * width, transcendentals=0),
        name="finish",
    )(operands[0], *results)


def solution(mesh):
    owned = P(("dp", "mp"), None, None)
    return jax.shard_map(
        functools.partial(body, mesh.shape["dp"], mesh.shape["mp"]),
        mesh=mesh,
        in_specs=(P(None, "dp", "mp"), P(), owned, owned, owned, owned),
        out_specs=(owned, owned, P(None, "dp", "mp")),
        check_vma=False,
    )
```

```python
import functools

import jax
import jax.numpy as jnp
from jax import lax
from jax.experimental import pallas as pl
from jax.experimental.pallas import tpu as pltpu
from jax.sharding import PartitionSpec as P

MESH = pl.DeviceIdType.MESH
F32 = jnp.float32
BF16 = jnp.bfloat16
beta_two = 0.95
clip_rms = 0.5


def fold(x):
    x = x.astype(F32)
    return jnp.sum((x * x).reshape(-1, 8, 128), axis=0)


def everything(x):
    return jnp.sum(jnp.sum(x, axis=0, keepdims=True), axis=1, keepdims=True)


def kernel(
    nd,
    nm,
    order_in,
    grads_in,
    left_stat,
    right_stat,
    left_root,
    right_root,
    new_left,
    new_right,
    u_in,
    scales,
    order,
    grads,
    tiles,
    slabs,
    full,
    lroot,
    rroot,
    acc,
    last_a,
    u_out,
    relay,
    columns,
    sq_dp,
    sq_mine,
    sq_mp,
    g_sq,
    sums,
    load_sem,
    slab_sem,
    tile_sem,
    forward_sem,
    root_sem,
    sq_send_sem,
    sq_recv_sem,
    sum_send_sem,
    sum_recv_sem,
    u_send_sem,
    u_recv_sem,
    relay_sem,
    column_send_sem,
    column_sem,
    ready_sem,
):
    blocks, rows, cols = grads.shape
    half, width = lroot.shape
    pairs = nm // 2
    d = lax.axis_index("dp")
    m = lax.axis_index("mp")
    h = m % 2
    pair = m // 2
    sigma = 2 * h - 1
    partner = m - sigma
    per_half = nd // 2
    my_rows = pl.ds(pl.multiple_of(h * half, half), half)

    def place(offset):
        return (m + offset + 2 * nm) % nm

    first_loads = [
        pltpu.make_async_copy(order_in.at[0], order, load_sem.at[4]),
        pltpu.make_async_copy(grads_in, grads, load_sem.at[5]),
    ]
    for load in first_loads:
        load.start()

    barrier = pltpu.get_barrier_semaphore()

    def greet(k, carry):
        pl.semaphore_signal(barrier, inc=1, device_id=((d + k) % nd, m), device_id_type=MESH)
        return carry

    lax.fori_loop(1, nd, greet, 0)
    for k in range(1, nm):
        pl.semaphore_signal(barrier, inc=1, device_id=(d, (m + k) % nm), device_id_type=MESH)

    loads = [
        pltpu.make_async_copy(left_root.at[0], lroot, load_sem.at[0]),
        pltpu.make_async_copy(right_root.at[0], rroot.at[my_rows], load_sem.at[1]),
        pltpu.make_async_copy(left_stat, new_left, load_sem.at[2]),
        pltpu.make_async_copy(right_stat, new_right, load_sem.at[3]),
    ]

    pl.semaphore_wait(barrier, nd - 1 + nm - 1)
    for k in range(1, nm):
        pl.semaphore_signal(ready_sem, inc=1, device_id=(d, (m + k) % nm), device_id_type=MESH)

    part_rows = half // 4

    def root_copy(n):
        return pltpu.make_async_remote_copy(
            src_ref=right_root.at[0, pl.ds(n * part_rows, part_rows)],
            dst_ref=rroot.at[pl.ds(pl.multiple_of(h * half + n * part_rows, part_rows), part_rows)],
            send_sem=root_sem.at[0],
            recv_sem=root_sem.at[1],
            device_id=(d, partner),
            device_id_type=MESH,
        )

    root_copy(0).start()
    for load in loads:
        load.start()

    targets = [place(3 * sigma), place(-2 * sigma), place(sigma), m]

    def tile_copy(there, target):
        return pltpu.make_async_remote_copy(
            src_ref=tiles.at[pairs * there + target // 2],
            dst_ref=slabs.at[m, pl.ds(pl.multiple_of(d * rows, rows), rows)],
            send_sem=tile_sem,
            recv_sem=slab_sem.at[m],
            device_id=(there, target),
            device_id_type=MESH,
        )

    def arrange(there, total):
        for p in range(pairs):
            s = pairs * there + p
            tile = grads[order[s]]
            tiles[s] = tile
            total = total + fold(tile)
        return total

    for load in first_loads:
        load.wait()
    pl.semaphore_wait(ready_sem, nm - 1)
    total = arrange(d, jnp.zeros((8, 128), F32))
    for target in targets[:3]:
        tile_copy(d, target).start()
    pltpu.make_async_copy(
        tiles.at[pairs * d + pair],
        slabs.at[m, pl.ds(pl.multiple_of(d * rows, rows), rows)],
        slab_sem.at[m],
    ).start()

    def send_tiles(k, total):
        there = (d + k) % nd
        total = arrange(there, total)
        for target in targets:
            tile_copy(there, target).start()
        return total

    sq_dp[d] = lax.fori_loop(1, nd, send_tiles, total)

    for n in range(1, 4):
        root_copy(n).start()

    def send_sq(k, carry):
        pltpu.make_async_remote_copy(
            src_ref=sq_dp.at[d],
            dst_ref=sq_dp.at[d],
            send_sem=sq_send_sem.at[0],
            recv_sem=sq_recv_sem.at[0],
            device_id=((d + k) % nd, m),
            device_id_type=MESH,
        ).start()
        return carry

    lax.fori_loop(1, nd, send_sq, 0)
    some = sq_dp.at[pl.ds(0, nd - 1)]
    pltpu.make_async_copy(some, some, sq_recv_sem.at[0]).wait()
    sq_mine[...] = jnp.sum(sq_dp[...], axis=0)
    sq_mp[m] = sq_mine[...]
    for k in range(1, nm):
        pltpu.make_async_remote_copy(
            src_ref=sq_mine,
            dst_ref=sq_mp.at[m],
            send_sem=sq_send_sem.at[1],
            recv_sem=sq_recv_sem.at[1],
            device_id=(d, (m + k) % nm),
            device_id_type=MESH,
        ).start()

    def wait_slab(k):
        pltpu.make_async_copy(slabs.at[k], slabs.at[k], slab_sem.at[k]).wait()

    def forward(k):
        return pltpu.make_async_remote_copy(
            src_ref=slabs.at[k],
            dst_ref=slabs.at[k],
            send_sem=forward_sem.at[k],
            recv_sem=slab_sem.at[k],
            device_id=(d, partner),
            device_id_type=MESH,
        )

    for j in range(pairs):
        k = place(j * sigma)
        wait_slab(k)
        forward(k).start()

    loads[0].wait()
    loads[1].wait()
    pltpu.make_async_copy(lroot, lroot, root_sem.at[1]).wait()
    acc[...] = jnp.zeros_like(acc)
    g_sq[...] = jnp.zeros_like(g_sq)

    def through_left(k):
        slab = slabs[k]
        g_sq[...] += fold(slab)
        return jnp.dot(lroot[...], slab, preferred_element_type=F32).astype(BF16)

    def right_rows(k):
        return pl.ds(pl.multiple_of(k * cols, cols), cols)

    def use_slab(k):
        a = through_left(k)
        acc[...] += jnp.dot(a, rroot[right_rows(k)], preferred_element_type=F32)

    def near(j, carry):
        use_slab(place(j * sigma))
        return carry

    def far(j, carry):
        k = place(-(j + 1) * sigma)
        wait_slab(k)
        use_slab(k)
        return carry

    lax.fori_loop(0, pairs, near, 0)
    lax.fori_loop(0, pairs - 1, far, 0)
    last = place(-pairs * sigma)
    wait_slab(last)
    last_a[...] = through_left(last)
    step = 2 * cols

    def finish(n, total):
        part = pl.ds(pl.multiple_of(n * step, step), step)
        u = acc[:, part] + jnp.dot(
            last_a[...], rroot[right_rows(last), part], preferred_element_type=F32
        )
        u_out[2 * n] = u[:, :cols].astype(BF16)
        u_out[2 * n + 1] = u[:, cols:].astype(BF16)
        return total + fold(u[:, :cols]) + fold(u[:, cols:])

    u_sq = lax.fori_loop(0, pairs, finish, jnp.zeros((8, 128), F32))

    row = lax.broadcasted_iota(jnp.int32, (8, 128), 0)
    sums[m] = jnp.where(row < 4, everything(u_sq), everything(g_sq[...]))
    for k in range(1, nm):
        pltpu.make_async_remote_copy(
            src_ref=sums.at[m],
            dst_ref=sums.at[m],
            send_sem=sum_send_sem.at[0],
            recv_sem=sum_recv_sem.at[0],
            device_id=(d, (m + k) % nm),
            device_id_type=MESH,
        ).start()

    opposite = place(nm // 2)
    chunks = min(4, per_half)
    chunk_places = per_half // chunks
    chunk_rows = half // chunks

    def chunk_at(i):
        c = (i + d // 2 + d // 8) % chunks
        return c, pl.ds(pl.multiple_of(c * chunk_rows, chunk_rows), chunk_rows)

    own_copy = pltpu.make_async_copy(u_out.at[m], columns.at[h, pair], load_sem.at[6])
    own_copy.start()

    def send_columns(i, carry):
        c, part = chunk_at(i)
        pltpu.make_async_remote_copy(
            src_ref=u_out.at[opposite, part],
            dst_ref=relay.at[part],
            send_sem=column_send_sem,
            recv_sem=relay_sem.at[c],
            device_id=(d, partner),
            device_id_type=MESH,
        ).start()
        for j in (3, 5, 2, 6, 1, 7):
            target = (m + j) % nm
            pltpu.make_async_remote_copy(
                src_ref=u_out.at[target, part],
                dst_ref=columns.at[h, pair, part],
                send_sem=column_send_sem,
                recv_sem=column_sem.at[m, c],
                device_id=(d, target),
                device_id_type=MESH,
            ).start()
        return carry

    lax.fori_loop(0, chunks, send_columns, 0)

    def pass_on(i, carry):
        c, part = chunk_at(i)
        pltpu.make_async_copy(relay.at[part], relay.at[part], relay_sem.at[c]).wait()
        pltpu.make_async_remote_copy(
            src_ref=relay.at[part],
            dst_ref=columns.at[1 - h, pair, part],
            send_sem=column_send_sem,
            recv_sem=column_sem.at[partner, c],
            device_id=(d, (partner + nm // 2) % nm),
            device_id_type=MESH,
        ).start()
        return carry

    def send_rows(i, carry):
        c, part = chunk_at(i)
        for j in range(1, nm):
            landed = columns.at[0, 0, part]
            pltpu.make_async_copy(landed, landed, column_sem.at[(m + j) % nm, c]).wait()
        for side in range(2):
            for n in range(chunk_places):
                near_row = c * chunk_places + (n + d) % chunk_places
                there = side * per_half + near_row
                tiles_there = columns.at[side, :, pl.ds(pl.multiple_of(near_row * rows, rows), rows)]
                place_there = u_in.at[pl.ds(pairs * d, pairs)]

                @pl.when(there == d)
                def _():
                    pltpu.make_async_copy(tiles_there, place_there, u_recv_sem).start()

                @pl.when(there != d)
                def _():
                    pltpu.make_async_remote_copy(
                        src_ref=tiles_there,
                        dst_ref=place_there,
                        send_sem=u_send_sem,
                        recv_sem=u_recv_sem,
                        device_id=(there, m),
                        device_id_type=MESH,
                    ).start()
        return carry

    for k in range(nm):
        full[:, k * cols : (k + 1) * cols] = slabs[k]
    pass_on(0, 0)

    some_mp = sq_mp.at[pl.ds(0, nm - 1)]
    pltpu.make_async_copy(some_mp, some_mp, sq_recv_sem.at[1]).wait()
    total_sq = everything(jnp.sum(sq_mp[...], axis=0))
    clip = jnp.minimum(1.0, clip_rms * jnp.sqrt(F32(blocks * width * width)) / jnp.sqrt(total_sq + 1e-06))
    coefficient = (1.0 - beta_two) * clip * clip
    pltpu.make_async_copy(some_mp, some_mp, sum_recv_sem.at[0]).wait()
    mine = jnp.zeros((8, 128), F32)
    for p in range(pairs):
        u_total = sums[2 * p, 0:1] + sums[2 * p + 1, 0:1]
        scale = -(clip * jnp.sqrt(sums[2 * p, 4:5]) / jnp.sqrt(u_total + 1e-06))
        mine = jnp.where(row == p, scale, mine)
    scales[d] = mine

    def send_scales(k, carry):
        pltpu.make_async_remote_copy(
            src_ref=scales.at[d],
            dst_ref=scales.at[d],
            send_sem=sum_send_sem.at[1],
            recv_sem=sum_recv_sem.at[1],
            device_id=((d + k) % nd, m),
            device_id_type=MESH,
        ).start()
        return carry

    lax.fori_loop(1, nd, send_scales, 0)
    loads[2].wait()

    def left_gram(n, carry):
        part = pl.ds(pl.multiple_of(n * step, step), step)
        gram = lax.dot_general(
            full[my_rows], full[part], (((1,), (1,)), ((), ())), preferred_element_type=F32
        )
        new_left[0, :, part] = beta_two * new_left[0, :, part] + coefficient * gram
        return carry

    lax.fori_loop(0, width // step, left_gram, 0)
    if chunks > 1:
        pass_on(1, 0)
    own_copy.wait()
    send_rows(0, 0)
    loads[3].wait()

    def right_gram(n, carry):
        part = pl.ds(pl.multiple_of(n * step, step), step)
        gram = lax.dot_general(
            full[:, my_rows], full[:, part], (((0,), (0,)), ((), ())), preferred_element_type=F32
        )
        new_right[0, :, part] = beta_two * new_right[0, :, part] + coefficient * gram
        return carry

    lax.fori_loop(0, width // step, right_gram, 0)
    if chunks > 1:

        def both(i, carry):
            pass_on(i + 1, 0)
            return send_rows(i, carry)

        lax.fori_loop(1, chunks - 1, both, 0)
        send_rows(chunks - 1, 0)

    sent = tiles.at[pl.ds(0, blocks - 1)]
    pltpu.make_async_copy(sent, sent, tile_sem).wait()
    pltpu.make_async_copy(lroot, lroot, root_sem.at[0]).wait()
    pltpu.make_async_copy(some, some, sq_send_sem.at[0]).wait()
    pltpu.make_async_copy(some_mp, some_mp, sq_send_sem.at[1]).wait()
    pltpu.make_async_copy(some_mp, some_mp, sum_send_sem.at[0]).wait()
    pltpu.make_async_copy(some, some, sum_send_sem.at[1]).wait()
    for j in range(pairs):
        forward(place(j * sigma)).wait_send()

    sent = tiles.at[pl.ds(0, blocks - pairs)]
    pltpu.make_async_copy(sent, sent, u_send_sem).wait()
    pltpu.make_async_copy(u_out, u_out, column_send_sem).wait()
    pltpu.make_async_copy(some, some, sum_recv_sem.at[1]).wait()
    pltpu.make_async_copy(u_in, u_in, u_recv_sem).wait()


def finish_kernel(order_in, left, right, tiles, scales, new_left, new_right, update, order, arranged, sem):
    blocks = tiles.shape[0]
    pairs = blocks // scales.shape[0]
    order_copy = pltpu.make_async_copy(order_in.at[0], order, sem.at[0])
    order_copy.start()
    stores = [
        pltpu.make_async_copy(left, new_left, sem.at[1]),
        pltpu.make_async_copy(right, new_right, sem.at[2]),
    ]
    for store in stores:
        store.start()
    order_copy.wait()

    def give(there, carry):
        for p in range(pairs):
            s = pairs * there + p
            arranged[order[s]] = (tiles[s].astype(F32) * scales[there, p : p + 1]).astype(BF16)
        return carry

    lax.fori_loop(0, scales.shape[0], give, 0, unroll=2)
    last = pltpu.make_async_copy(arranged, update, sem.at[3])
    last.start()
    last.wait()
    for store in stores:
        store.wait()


def body(nd, nm, grads, order, left_stat, right_stat, left_root, right_root):
    blocks, rows, cols = grads.shape
    _, half, width = left_stat.shape
    vmem = pl.BlockSpec(memory_space=pltpu.VMEM)
    half_shape = left_stat.shape
    hbm = pl.BlockSpec(memory_space=pltpu.HBM)
    dma = pltpu.SemaphoreType.DMA
    operands = [order.reshape(1, blocks), grads, left_stat, right_stat, left_root, right_root]
    operands = [pltpu.with_memory_space_constraint(x, pltpu.HBM) for x in operands]
    products = 4 * half * width * width
    results = pl.pallas_call(
        functools.partial(kernel, nd, nm),
        out_shape=(
            pltpu.VMEM(left_stat.shape, F32),
            pltpu.VMEM(right_stat.shape, F32),
            pltpu.VMEM(grads.shape, BF16),
            pltpu.VMEM((nd, 8, 128), F32),
        ),
        in_specs=[hbm] * 6,
        out_specs=(vmem, vmem, vmem, vmem),
        scratch_shapes=[
            pltpu.SMEM((blocks,), jnp.int32),
            pltpu.VMEM((blocks, rows, cols), BF16),
            pltpu.VMEM((blocks, rows, cols), BF16),
            pltpu.VMEM((nm, width, cols), BF16),
            pltpu.VMEM((width, width), BF16),
            pltpu.VMEM((half, width), BF16),
            pltpu.VMEM((width, width), BF16),
            pltpu.VMEM((half, width), F32),
            pltpu.VMEM((half, cols), BF16),
            pltpu.VMEM((nm, half, cols), BF16),
            pltpu.VMEM((half, cols), BF16),
            pltpu.VMEM((2, nm // 2, half, cols), BF16),
            pltpu.VMEM((nd, 8, 128), F32),
            pltpu.VMEM((8, 128), F32),
            pltpu.VMEM((nm, 8, 128), F32),
            pltpu.VMEM((8, 128), F32),
            pltpu.VMEM((nm, 8, 128), F32),
            dma((7,)),
            dma((nm,)),
            dma,
            dma((nm,)),
            dma((2,)),
            dma((2,)),
            dma((2,)),
            dma((2,)),
            dma((2,)),
            dma,
            dma,
            dma((4,)),
            dma,
            dma((nm, 4)),
            pltpu.SemaphoreType.REGULAR,
        ],
        compiler_params=pltpu.CompilerParams(
            collective_id=0, has_side_effects=True, vmem_limit_bytes=48 * 1024 * 1024
        ),
        cost_estimate=pl.CostEstimate(
            flops=2 * products, bytes_accessed=12 * half * width * 2, transcendentals=0
        ),
        name="step",
    )(*operands)
    return pl.pallas_call(
        finish_kernel,
        out_shape=(
            pltpu.HBM(half_shape, F32),
            pltpu.HBM(half_shape, F32),
            pltpu.HBM(grads.shape, BF16),
        ),
        in_specs=[hbm, vmem, vmem, vmem, vmem],
        out_specs=(hbm, hbm, hbm),
        scratch_shapes=[
            pltpu.SMEM((blocks,), jnp.int32),
            pltpu.VMEM(grads.shape, BF16),
            dma((4,)),
        ],
        compiler_params=pltpu.CompilerParams(vmem_limit_bytes=8 * 1024 * 1024),
        cost_estimate=pl.CostEstimate(flops=0, bytes_accessed=10 * half * width, transcendentals=0),
        name="finish",
    )(operands[0], *results)


def solution(mesh):
    owned = P(("dp", "mp"), None, None)
    return jax.shard_map(
        functools.partial(body, mesh.shape["dp"], mesh.shape["mp"]),
        mesh=mesh,
        in_specs=(P(None, "dp", "mp"), P(), owned, owned, owned, owned),
        out_specs=(owned, owned, P(None, "dp", "mp")),
        check_vma=False,
    )
```

```python
import functools

import jax
import jax.numpy as jnp
from jax import lax
from jax.experimental import pallas as pl
from jax.experimental.pallas import tpu as pltpu
from jax.sharding import PartitionSpec as P

MESH = pl.DeviceIdType.MESH
F32 = jnp.float32
BF16 = jnp.bfloat16
beta_two = 0.95
clip_rms = 0.5


def fold(x):
    x = x.astype(F32)
    return jnp.sum((x * x).reshape(-1, 8, 128), axis=0)


def everything(x):
    return jnp.sum(jnp.sum(x, axis=0, keepdims=True), axis=1, keepdims=True)


def kernel(
    nd,
    nm,
    order_in,
    grads_in,
    left_stat,
    right_stat,
    left_root,
    right_root,
    new_left,
    new_right,
    u_in,
    scales,
    order_row,
    order,
    grads,
    tiles,
    slabs,
    full,
    lroot,
    rroot,
    product,
    u_out,
    sq_dp,
    sq_mine,
    sq_mp,
    g_sq,
    sums,
    load_sem,
    slab_sem,
    tile_sem,
    forward_sem,
    root_send_sem,
    root_sem,
    sq_send_sem,
    sq_recv_sem,
    sum_send_sem,
    sum_recv_sem,
    u_send_sem,
    u_recv_sem,
    ready_sem,
):
    blocks, rows, cols = grads.shape
    half, width = lroot.shape
    pairs = nm // 2
    d = lax.axis_index("dp")
    m = lax.axis_index("mp")
    h = m % 2
    pair = m // 2
    sigma = 2 * h - 1
    partner = m - sigma
    per_half = nd // 2
    my_rows = pl.ds(pl.multiple_of(h * half, half), half)

    def place(offset):
        return (m + offset + 2 * nm) % nm

    first_loads = [
        pltpu.make_async_copy(order_in.at[0], order, load_sem.at[4]),
        pltpu.make_async_copy(grads_in, grads, load_sem.at[5]),
        pltpu.make_async_copy(order_in, order_row, load_sem.at[6]),
    ]
    for load in first_loads:
        load.start()

    barrier = pltpu.get_barrier_semaphore()

    def greet(k, carry):
        pl.semaphore_signal(barrier, inc=1, device_id=((d + k) % nd, m), device_id_type=MESH)
        return carry

    lax.fori_loop(1, nd, greet, 0)
    for k in range(1, nm):
        pl.semaphore_signal(barrier, inc=1, device_id=(d, (m + k) % nm), device_id_type=MESH)

    loads = [
        pltpu.make_async_copy(left_root.at[0], lroot, load_sem.at[0]),
        pltpu.make_async_copy(right_root.at[0], rroot.at[my_rows], load_sem.at[1]),
        pltpu.make_async_copy(left_stat, new_left, load_sem.at[2]),
        pltpu.make_async_copy(right_stat, new_right, load_sem.at[3]),
    ]

    pl.semaphore_wait(barrier, nd - 1 + nm - 1)
    for k in range(1, nm):
        pl.semaphore_signal(ready_sem, inc=1, device_id=(d, (m + k) % nm), device_id_type=MESH)

    def root_copy(i):
        part = pl.ds(i * cols, cols)
        return pltpu.make_async_remote_copy(
            src_ref=right_root.at[0, :, part],
            dst_ref=rroot.at[my_rows, part],
            send_sem=root_send_sem,
            recv_sem=root_sem,
            device_id=(d, partner),
            device_id_type=MESH,
        )

    root_copy(0).start()
    for load in loads:
        load.start()

    targets = [place(3 * sigma), place(-2 * sigma), place(sigma), m]

    def tile_copy(there, target):
        return pltpu.make_async_remote_copy(
            src_ref=tiles.at[pairs * there + target // 2],
            dst_ref=slabs.at[m, pl.ds(pl.multiple_of(d * rows, rows), rows)],
            send_sem=tile_sem,
            recv_sem=slab_sem.at[m],
            device_id=(there, target),
            device_id_type=MESH,
        )

    def arrange(there, total):
        for p in range(pairs):
            s = pairs * there + p
            tile = grads[order[s]]
            tiles[s] = tile
            total = total + fold(tile)
        return total

    for load in first_loads[:2]:
        load.wait()
    pl.semaphore_wait(ready_sem, nm - 1)
    total = arrange(d, jnp.zeros((8, 128), F32))
    for target in targets[:3]:
        tile_copy(d, target).start()
    pltpu.make_async_copy(
        tiles.at[pairs * d + pair],
        slabs.at[m, pl.ds(pl.multiple_of(d * rows, rows), rows)],
        slab_sem.at[m],
    ).start()

    def send_tiles(k, total):
        there = (d + k) % nd
        total = arrange(there, total)
        for target in targets:
            tile_copy(there, target).start()
        return total

    for i in range(pairs):
        if i > 0:
            root_copy(i).start()
        total = lax.fori_loop(max(1, i * nd // pairs), (i + 1) * nd // pairs, send_tiles, total)
    sq_dp[d] = total

    def send_sq(k, carry):
        pltpu.make_async_remote_copy(
            src_ref=sq_dp.at[d],
            dst_ref=sq_dp.at[d],
            send_sem=sq_send_sem.at[0],
            recv_sem=sq_recv_sem.at[0],
            device_id=((d + k) % nd, m),
            device_id_type=MESH,
        ).start()
        return carry

    lax.fori_loop(1, nd, send_sq, 0)
    some = sq_dp.at[pl.ds(0, nd - 1)]
    pltpu.make_async_copy(some, some, sq_recv_sem.at[0]).wait()
    sq_mine[...] = jnp.sum(sq_dp[...], axis=0)
    sq_mp[m] = sq_mine[...]
    for k in range(1, nm):
        pltpu.make_async_remote_copy(
            src_ref=sq_mine,
            dst_ref=sq_mp.at[m],
            send_sem=sq_send_sem.at[1],
            recv_sem=sq_recv_sem.at[1],
            device_id=(d, (m + k) % nm),
            device_id_type=MESH,
        ).start()

    def wait_slab(k):
        pltpu.make_async_copy(slabs.at[k], slabs.at[k], slab_sem.at[k]).wait()

    def forward(k):
        return pltpu.make_async_remote_copy(
            src_ref=slabs.at[k],
            dst_ref=slabs.at[k],
            send_sem=forward_sem.at[k],
            recv_sem=slab_sem.at[k],
            device_id=(d, partner),
            device_id_type=MESH,
        )

    for j in range(pairs):
        k = place(j * sigma)
        wait_slab(k)
        forward(k).start()
        root_copy(pairs + j).start()

    loads[0].wait()
    g_sq[...] = jnp.zeros_like(g_sq)

    def through_left(k):
        slab = slabs[k]
        a = jnp.dot(lroot[...], slab, preferred_element_type=F32).astype(BF16)
        product[:, pl.ds(pl.multiple_of(k * cols, cols), cols)] = a
        g_sq[...] += fold(slab)

    def near(j, carry):
        through_left(place(j * sigma))
        return carry

    def far(j, carry):
        k = place(-(j + 1) * sigma)
        wait_slab(k)
        through_left(k)
        return carry

    lax.fori_loop(0, pairs, near, 0)
    lax.fori_loop(0, pairs - 1, far, 0)
    last = place(-pairs * sigma)
    wait_slab(last)
    through_left(last)
    loads[1].wait()
    pltpu.make_async_copy(lroot, lroot, root_sem).wait()

    slot = pairs * d + pair
    own_half = d // per_half == h

    step = 2 * cols

    def chunk(i):
        n = (pair + (2, 1, 3, 0)[i]) % pairs
        return n, pl.ds(pl.multiple_of(n * step, step), step)

    def work_out(i):
        n, part = chunk(i)
        u = jnp.dot(product[...], rroot[:, part], preferred_element_type=F32)
        u_out[2 * n] = u[:, :cols].astype(BF16)
        u_out[2 * n + 1] = u[:, cols:].astype(BF16)
        return fold(u[:, :cols]) + fold(u[:, cols:])

    def u_copy(near_row, target):
        return pltpu.make_async_remote_copy(
            src_ref=u_out.at[target, pl.ds(pl.multiple_of(near_row * rows, rows), rows)],
            dst_ref=u_in.at[slot],
            send_sem=u_send_sem,
            recv_sem=u_recv_sem,
            device_id=(h * per_half + near_row, target),
            device_id_type=MESH,
        )

    def send_far(i):
        n, _ = chunk(i)

        def send(k, carry):
            near_row = (d + k) % per_half
            for side in range(2):
                u_copy(near_row, 2 * n + side).start()
            return carry

        lax.fori_loop(0, per_half, send, 0)

    def send_near(k, carry):
        near_row = (d + k) % per_half
        u_copy(near_row, partner).start()
        here = jnp.logical_and(own_half, k == 0)

        @pl.when(here)
        def _():
            pltpu.make_async_copy(
                u_out.at[m, pl.ds(pl.multiple_of(near_row * rows, rows), rows)],
                u_in.at[slot],
                u_recv_sem,
            ).start()

        @pl.when(jnp.logical_not(here))
        def _():
            u_copy(near_row, m).start()

        return carry

    u_sq = work_out(0)
    send_far(0)
    for i in range(1, pairs):
        u_sq = u_sq + work_out(i)

    row = lax.broadcasted_iota(jnp.int32, (8, 128), 0)
    sums[m] = jnp.where(row < 4, everything(u_sq), everything(g_sq[...]))
    for k in range(1, nm):
        pltpu.make_async_remote_copy(
            src_ref=sums.at[m],
            dst_ref=sums.at[m],
            send_sem=sum_send_sem.at[0],
            recv_sem=sum_recv_sem.at[0],
            device_id=(d, (m + k) % nm),
            device_id_type=MESH,
        ).start()
    for i in range(1, pairs - 1):
        send_far(i)

    some_mp = sq_mp.at[pl.ds(0, nm - 1)]
    pltpu.make_async_copy(some_mp, some_mp, sq_recv_sem.at[1]).wait()
    total_sq = everything(jnp.sum(sq_mp[...], axis=0))
    clip = jnp.minimum(1.0, clip_rms * jnp.sqrt(F32(blocks * width * width)) / jnp.sqrt(total_sq + 1e-06))
    coefficient = (1.0 - beta_two) * clip * clip
    pltpu.make_async_copy(some_mp, some_mp, sum_recv_sem.at[0]).wait()
    mine = jnp.zeros((8, 128), F32)
    for p in range(pairs):
        u_total = sums[2 * p, 0:1] + sums[2 * p + 1, 0:1]
        scale = -(clip * jnp.sqrt(sums[2 * p, 4:5]) / jnp.sqrt(u_total + 1e-06))
        mine = jnp.where(row == p, scale, mine)
    scales[d] = mine

    def send_scales(k, carry):
        pltpu.make_async_remote_copy(
            src_ref=scales.at[d],
            dst_ref=scales.at[d],
            send_sem=sum_send_sem.at[1],
            recv_sem=sum_recv_sem.at[1],
            device_id=((d + k) % nd, m),
            device_id_type=MESH,
        ).start()
        return carry

    lax.fori_loop(1, nd, send_scales, 0)
    lax.fori_loop(0, per_half, send_near, 0)

    for k in range(nm):
        full[:, k * cols : (k + 1) * cols] = slabs[k]
    loads[2].wait()

    def left_gram(n, carry):
        part = pl.ds(pl.multiple_of(n * step, step), step)
        gram = lax.dot_general(
            full[my_rows], full[part], (((1,), (1,)), ((), ())), preferred_element_type=F32
        )
        new_left[0, :, part] = beta_two * new_left[0, :, part] + coefficient * gram
        return carry

    lax.fori_loop(0, width // step, left_gram, 0)
    loads[3].wait()

    def right_gram(n, carry):
        part = pl.ds(pl.multiple_of(n * step, step), step)
        gram = lax.dot_general(
            full[:, my_rows], full[:, part], (((0,), (0,)), ((), ())), preferred_element_type=F32
        )
        new_right[0, :, part] = beta_two * new_right[0, :, part] + coefficient * gram
        return carry

    lax.fori_loop(0, width // step, right_gram, 0)

    first_loads[2].wait()
    sent = tiles.at[pl.ds(0, blocks - 1)]
    pltpu.make_async_copy(sent, sent, tile_sem).wait()
    pltpu.make_async_copy(lroot, lroot, root_send_sem).wait()
    pltpu.make_async_copy(some, some, sq_send_sem.at[0]).wait()
    pltpu.make_async_copy(some_mp, some_mp, sq_send_sem.at[1]).wait()
    pltpu.make_async_copy(some_mp, some_mp, sum_send_sem.at[0]).wait()
    pltpu.make_async_copy(some, some, sum_send_sem.at[1]).wait()
    for j in range(pairs):
        forward(place(j * sigma)).wait_send()

    @pl.when(own_half)
    def _():
        pltpu.make_async_copy(sent, sent, u_send_sem).wait()

    @pl.when(jnp.logical_not(own_half))
    def _():
        pltpu.make_async_copy(tiles, tiles, u_send_sem).wait()

    pltpu.make_async_copy(some, some, sum_recv_sem.at[1]).wait()
    pltpu.make_async_copy(u_in, u_in, u_recv_sem).wait()


def finish_kernel(left, right, tiles, scales, order_in, new_left, new_right, update, order, arranged, sem):
    places = scales.shape[0]
    pairs = tiles.shape[0] // places
    order_copy = pltpu.make_async_copy(order_in.at[0], order, sem.at[0])
    order_copy.start()
    stores = [
        pltpu.make_async_copy(left, new_left, sem.at[1]),
        pltpu.make_async_copy(right, new_right, sem.at[2]),
        pltpu.make_async_copy(arranged, update, sem.at[3]),
    ]
    for store in stores[:2]:
        store.start()
    order_copy.wait()

    def give(there, carry):
        for p in range(pairs):
            s = pairs * there + p
            arranged[order[s]] = (tiles[s].astype(F32) * scales[there, p : p + 1]).astype(BF16)
        return carry

    lax.fori_loop(0, places, give, 0, unroll=2)
    stores[2].start()
    for store in stores:
        store.wait()


def body(nd, nm, grads, order, left_stat, right_stat, left_root, right_root):
    blocks, rows, cols = grads.shape
    _, half, width = left_stat.shape
    vmem = pl.BlockSpec(memory_space=pltpu.VMEM)
    half_shape = left_stat.shape
    hbm = pl.BlockSpec(memory_space=pltpu.HBM)
    dma = pltpu.SemaphoreType.DMA
    operands = [order.reshape(1, blocks), grads, left_stat, right_stat, left_root, right_root]
    operands = [pltpu.with_memory_space_constraint(x, pltpu.HBM) for x in operands]
    products = 4 * half * width * width
    results = pl.pallas_call(
        functools.partial(kernel, nd, nm),
        out_shape=(
            pltpu.VMEM(left_stat.shape, F32),
            pltpu.VMEM(right_stat.shape, F32),
            pltpu.VMEM(grads.shape, BF16),
            pltpu.VMEM((nd, 8, 128), F32),
            pltpu.VMEM((1, blocks), jnp.int32),
        ),
        in_specs=[hbm] * 6,
        out_specs=(vmem,) * 5,
        scratch_shapes=[
            pltpu.SMEM((blocks,), jnp.int32),
            pltpu.VMEM((blocks, rows, cols), BF16),
            pltpu.VMEM((blocks, rows, cols), BF16),
            pltpu.VMEM((nm, width, cols), BF16),
            pltpu.VMEM((width, width), BF16),
            pltpu.VMEM((half, width), BF16),
            pltpu.VMEM((width, width), BF16),
            pltpu.VMEM((half, width), BF16),
            pltpu.VMEM((nm, half, cols), BF16),
            pltpu.VMEM((nd, 8, 128), F32),
            pltpu.VMEM((8, 128), F32),
            pltpu.VMEM((nm, 8, 128), F32),
            pltpu.VMEM((8, 128), F32),
            pltpu.VMEM((nm, 8, 128), F32),
            dma((7,)),
            dma((nm,)),
            dma,
            dma((nm,)),
            dma,
            dma,
            dma((2,)),
            dma((2,)),
            dma((2,)),
            dma((2,)),
            dma,
            dma,
            pltpu.SemaphoreType.REGULAR,
        ],
        compiler_params=pltpu.CompilerParams(
            collective_id=0, has_side_effects=True, vmem_limit_bytes=48 * 1024 * 1024
        ),
        cost_estimate=pl.CostEstimate(
            flops=2 * products, bytes_accessed=12 * half * width * 2, transcendentals=0
        ),
        name="step",
    )(*operands)
    return pl.pallas_call(
        finish_kernel,
        out_shape=(
            pltpu.HBM(half_shape, F32),
            pltpu.HBM(half_shape, F32),
            pltpu.HBM(grads.shape, BF16),
        ),
        in_specs=[vmem] * 5,
        out_specs=(hbm, hbm, hbm),
        scratch_shapes=[
            pltpu.SMEM((blocks,), jnp.int32),
            pltpu.VMEM(grads.shape, BF16),
            dma((4,)),
        ],
        compiler_params=pltpu.CompilerParams(vmem_limit_bytes=8 * 1024 * 1024),
        cost_estimate=pl.CostEstimate(flops=0, bytes_accessed=10 * half * width, transcendentals=0),
        name="finish",
    )(*results)


def solution(mesh):
    owned = P(("dp", "mp"), None, None)
    return jax.shard_map(
        functools.partial(body, mesh.shape["dp"], mesh.shape["mp"]),
        mesh=mesh,
        in_specs=(P(None, "dp", "mp"), P(), owned, owned, owned, owned),
        out_specs=(owned, owned, P(None, "dp", "mp")),
        check_vma=False,
    )
```

```python
import functools

import jax
import jax.numpy as jnp
from jax import lax
from jax.experimental import pallas as pl
from jax.experimental.pallas import tpu as pltpu
from jax.sharding import PartitionSpec as P

MESH = pl.DeviceIdType.MESH
F32 = jnp.float32
BF16 = jnp.bfloat16
beta_two = 0.95
clip_rms = 0.5


def fold(x):
    x = x.astype(F32)
    return jnp.sum((x * x).reshape(-1, 8, 128), axis=0)


def everything(x):
    return jnp.sum(jnp.sum(x, axis=0, keepdims=True), axis=1, keepdims=True)


def kernel(
    nd,
    nm,
    order_in,
    grads_in,
    left_stat,
    right_stat,
    left_root,
    right_root,
    new_left,
    new_right,
    u_in,
    scales,
    order,
    grads,
    tiles,
    slabs,
    full,
    lroot,
    rroot,
    acc,
    last_a,
    u_out,
    relay,
    sq_dp,
    sq_mine,
    sq_mp,
    g_sq,
    sums,
    load_sem,
    slab_sem,
    tile_sem,
    forward_sem,
    root_sem,
    sq_send_sem,
    sq_recv_sem,
    sum_send_sem,
    sum_recv_sem,
    u_send_sem,
    u_recv_sem,
    relay_sem,
    ready_sem,
):
    blocks, rows, cols = grads.shape
    half, width = lroot.shape
    pairs = nm // 2
    d = lax.axis_index("dp")
    m = lax.axis_index("mp")
    h = m % 2
    pair = m // 2
    sigma = 2 * h - 1
    partner = m - sigma
    per_half = nd // 2
    my_rows = pl.ds(pl.multiple_of(h * half, half), half)

    def place(offset):
        return (m + offset + 2 * nm) % nm

    first_loads = [
        pltpu.make_async_copy(order_in.at[0], order, load_sem.at[4]),
        pltpu.make_async_copy(grads_in, grads, load_sem.at[5]),
    ]
    for load in first_loads:
        load.start()

    barrier = pltpu.get_barrier_semaphore()

    def greet(k, carry):
        pl.semaphore_signal(barrier, inc=1, device_id=((d + k) % nd, m), device_id_type=MESH)
        return carry

    lax.fori_loop(1, nd, greet, 0)
    for k in range(1, nm):
        pl.semaphore_signal(barrier, inc=1, device_id=(d, (m + k) % nm), device_id_type=MESH)

    loads = [
        pltpu.make_async_copy(left_root.at[0], lroot, load_sem.at[0]),
        pltpu.make_async_copy(right_root.at[0], rroot.at[my_rows], load_sem.at[1]),
        pltpu.make_async_copy(left_stat, new_left, load_sem.at[2]),
        pltpu.make_async_copy(right_stat, new_right, load_sem.at[3]),
    ]

    pl.semaphore_wait(barrier, nd - 1 + nm - 1)
    for k in range(1, nm):
        pl.semaphore_signal(ready_sem, inc=1, device_id=(d, (m + k) % nm), device_id_type=MESH)

    part_rows = half // 4

    def root_copy(n):
        return pltpu.make_async_remote_copy(
            src_ref=right_root.at[0, pl.ds(n * part_rows, part_rows)],
            dst_ref=rroot.at[pl.ds(pl.multiple_of(h * half + n * part_rows, part_rows), part_rows)],
            send_sem=root_sem.at[0],
            recv_sem=root_sem.at[1],
            device_id=(d, partner),
            device_id_type=MESH,
        )

    root_copy(0).start()
    for load in loads:
        load.start()

    targets = [place(3 * sigma), place(-2 * sigma), place(sigma), m]

    def tile_copy(there, target):
        return pltpu.make_async_remote_copy(
            src_ref=tiles.at[pairs * there + target // 2],
            dst_ref=slabs.at[m, pl.ds(pl.multiple_of(d * rows, rows), rows)],
            send_sem=tile_sem,
            recv_sem=slab_sem.at[m],
            device_id=(there, target),
            device_id_type=MESH,
        )

    def arrange(there, total):
        for p in range(pairs):
            s = pairs * there + p
            tile = grads[order[s]]
            tiles[s] = tile
            total = total + fold(tile)
        return total

    for load in first_loads:
        load.wait()
    pl.semaphore_wait(ready_sem, nm - 1)
    total = arrange(d, jnp.zeros((8, 128), F32))
    for target in targets[:3]:
        tile_copy(d, target).start()
    pltpu.make_async_copy(
        tiles.at[pairs * d + pair],
        slabs.at[m, pl.ds(pl.multiple_of(d * rows, rows), rows)],
        slab_sem.at[m],
    ).start()

    def send_tiles(k, total):
        there = (d + 11 * k) % nd
        total = arrange(there, total)
        for target in targets:
            tile_copy(there, target).start()
        return total

    sq_dp[d] = lax.fori_loop(1, nd, send_tiles, total)

    for n in range(1, 4):
        root_copy(n).start()

    def send_sq(k, carry):
        pltpu.make_async_remote_copy(
            src_ref=sq_dp.at[d],
            dst_ref=sq_dp.at[d],
            send_sem=sq_send_sem.at[0],
            recv_sem=sq_recv_sem.at[0],
            device_id=((d + k) % nd, m),
            device_id_type=MESH,
        ).start()
        return carry

    lax.fori_loop(1, nd, send_sq, 0)
    some = sq_dp.at[pl.ds(0, nd - 1)]
    pltpu.make_async_copy(some, some, sq_recv_sem.at[0]).wait()
    sq_mine[...] = jnp.sum(sq_dp[...], axis=0)
    sq_mp[m] = sq_mine[...]
    for k in range(1, nm):
        pltpu.make_async_remote_copy(
            src_ref=sq_mine,
            dst_ref=sq_mp.at[m],
            send_sem=sq_send_sem.at[1],
            recv_sem=sq_recv_sem.at[1],
            device_id=(d, (m + k) % nm),
            device_id_type=MESH,
        ).start()

    def wait_slab(k):
        pltpu.make_async_copy(slabs.at[k], slabs.at[k], slab_sem.at[k]).wait()

    def forward(k):
        return pltpu.make_async_remote_copy(
            src_ref=slabs.at[k],
            dst_ref=slabs.at[k],
            send_sem=forward_sem.at[k],
            recv_sem=slab_sem.at[k],
            device_id=(d, partner),
            device_id_type=MESH,
        )

    for j in range(pairs):
        k = place(j * sigma)
        wait_slab(k)
        forward(k).start()

    loads[0].wait()
    loads[1].wait()
    pltpu.make_async_copy(lroot, lroot, root_sem.at[1]).wait()
    acc[...] = jnp.zeros_like(acc)
    g_sq[...] = jnp.zeros_like(g_sq)

    def through_left(k):
        slab = slabs[k]
        g_sq[...] += fold(slab)
        return jnp.dot(lroot[...], slab, preferred_element_type=F32).astype(BF16)

    def right_rows(k):
        return pl.ds(pl.multiple_of(k * cols, cols), cols)

    def use_slab(k):
        a = through_left(k)
        acc[...] += jnp.dot(a, rroot[right_rows(k)], preferred_element_type=F32)

    def near(j, carry):
        use_slab(place(j * sigma))
        return carry

    def far(j, carry):
        k = place(-(j + 1) * sigma)
        wait_slab(k)
        use_slab(k)
        return carry

    lax.fori_loop(0, pairs, near, 0)
    lax.fori_loop(0, pairs - 1, far, 0)
    last = place(-pairs * sigma)
    wait_slab(last)
    last_a[...] = through_left(last)
    step = 2 * cols

    opposite = place(nm // 2)

    def finish(i, total):
        n = (opposite // 2 + i) % pairs
        part = pl.ds(pl.multiple_of(n * step, step), step)
        u = acc[:, part] + jnp.dot(
            last_a[...], rroot[right_rows(last), part], preferred_element_type=F32
        )
        u_out[2 * n] = u[:, :cols].astype(BF16)
        u_out[2 * n + 1] = u[:, cols:].astype(BF16)
        return total + fold(u[:, :cols]) + fold(u[:, cols:])

    u_sq = finish(0, jnp.zeros((8, 128), F32))
    relay_copy = pltpu.make_async_remote_copy(
        src_ref=u_out.at[opposite],
        dst_ref=relay,
        send_sem=relay_sem.at[0],
        recv_sem=relay_sem.at[1],
        device_id=(d, partner),
        device_id_type=MESH,
    )
    relay_copy.start()
    u_sq = lax.fori_loop(1, pairs, finish, u_sq)

    row = lax.broadcasted_iota(jnp.int32, (8, 128), 0)
    sums[m] = jnp.where(row < 4, everything(u_sq), everything(g_sq[...]))
    for k in range(1, nm):
        pltpu.make_async_remote_copy(
            src_ref=sums.at[m],
            dst_ref=sums.at[m],
            send_sem=sum_send_sem.at[0],
            recv_sem=sum_recv_sem.at[0],
            device_id=(d, (m + k) % nm),
            device_id_type=MESH,
        ).start()

    slot = pairs * d + pair

    def u_copy(near_row, target):
        return pltpu.make_async_remote_copy(
            src_ref=u_out.at[target, pl.ds(pl.multiple_of(near_row * rows, rows), rows)],
            dst_ref=u_in.at[slot],
            send_sem=u_send_sem,
            recv_sem=u_recv_sem,
            device_id=(h * per_half + near_row, target),
            device_id_type=MESH,
        )

    own_half = d // per_half == h

    def send_u(k, carry):
        near_row = (d + 7 * k) % per_half
        for j in range(1, nm):
            if j != nm // 2:
                u_copy(near_row, (m + j) % nm).start()
        here = jnp.logical_and(own_half, k == 0)

        @pl.when(here)
        def _():
            pltpu.make_async_copy(
                u_out.at[m, pl.ds(pl.multiple_of(near_row * rows, rows), rows)],
                u_in.at[slot],
                u_recv_sem,
            ).start()

        @pl.when(jnp.logical_not(here))
        def _():
            u_copy(near_row, m).start()

        return carry

    lax.fori_loop(0, per_half // 2, send_u, 0)
    relay_copy.wait_recv()

    def pass_on(k, carry):
        near_row = (d + 7 * k) % per_half
        pltpu.make_async_remote_copy(
            src_ref=relay.at[pl.ds(pl.multiple_of(near_row * rows, rows), rows)],
            dst_ref=u_in.at[slot],
            send_sem=u_send_sem,
            recv_sem=u_recv_sem,
            device_id=((1 - h) * per_half + near_row, (partner + nm // 2) % nm),
            device_id_type=MESH,
        ).start()
        return carry

    lax.fori_loop(0, per_half, pass_on, 0)

    some_mp = sq_mp.at[pl.ds(0, nm - 1)]
    pltpu.make_async_copy(some_mp, some_mp, sq_recv_sem.at[1]).wait()
    total_sq = everything(jnp.sum(sq_mp[...], axis=0))
    clip = jnp.minimum(1.0, clip_rms * jnp.sqrt(F32(blocks * width * width)) / jnp.sqrt(total_sq + 1e-06))
    coefficient = (1.0 - beta_two) * clip * clip
    pltpu.make_async_copy(some_mp, some_mp, sum_recv_sem.at[0]).wait()
    mine = jnp.zeros((8, 128), F32)
    for p in range(pairs):
        u_total = sums[2 * p, 0:1] + sums[2 * p + 1, 0:1]
        scale = -(clip * jnp.sqrt(sums[2 * p, 4:5]) / jnp.sqrt(u_total + 1e-06))
        mine = jnp.where(row == p, scale, mine)
    scales[d] = mine

    def send_scales(k, carry):
        pltpu.make_async_remote_copy(
            src_ref=scales.at[d],
            dst_ref=scales.at[d],
            send_sem=sum_send_sem.at[1],
            recv_sem=sum_recv_sem.at[1],
            device_id=((d + k) % nd, m),
            device_id_type=MESH,
        ).start()
        return carry

    lax.fori_loop(1, nd, send_scales, 0)
    lax.fori_loop(per_half // 2, per_half, send_u, 0)

    for k in range(nm):
        full[:, k * cols : (k + 1) * cols] = slabs[k]
    loads[2].wait()

    def left_gram(n, carry):
        part = pl.ds(pl.multiple_of(n * step, step), step)
        gram = lax.dot_general(
            full[my_rows], full[part], (((1,), (1,)), ((), ())), preferred_element_type=F32
        )
        new_left[0, :, part] = beta_two * new_left[0, :, part] + coefficient * gram
        return carry

    lax.fori_loop(0, width // step, left_gram, 0)
    loads[3].wait()

    def right_gram(n, carry):
        part = pl.ds(pl.multiple_of(n * step, step), step)
        gram = lax.dot_general(
            full[:, my_rows], full[:, part], (((0,), (0,)), ((), ())), preferred_element_type=F32
        )
        new_right[0, :, part] = beta_two * new_right[0, :, part] + coefficient * gram
        return carry

    lax.fori_loop(0, width // step, right_gram, 0)

    sent = tiles.at[pl.ds(0, blocks - 1)]
    pltpu.make_async_copy(sent, sent, tile_sem).wait()
    pltpu.make_async_copy(lroot, lroot, root_sem.at[0]).wait()
    pltpu.make_async_copy(some, some, sq_send_sem.at[0]).wait()
    pltpu.make_async_copy(some_mp, some_mp, sq_send_sem.at[1]).wait()
    pltpu.make_async_copy(some_mp, some_mp, sum_send_sem.at[0]).wait()
    pltpu.make_async_copy(some, some, sum_send_sem.at[1]).wait()
    relay_copy.wait_send()
    for j in range(pairs):
        forward(place(j * sigma)).wait_send()

    @pl.when(own_half)
    def _():
        pltpu.make_async_copy(sent, sent, u_send_sem).wait()

    @pl.when(jnp.logical_not(own_half))
    def _():
        pltpu.make_async_copy(tiles, tiles, u_send_sem).wait()

    pltpu.make_async_copy(some, some, sum_recv_sem.at[1]).wait()
    pltpu.make_async_copy(u_in, u_in, u_recv_sem).wait()


def finish_kernel(order_in, left, right, tiles, scales, new_left, new_right, update, order, arranged, sem):
    blocks = tiles.shape[0]
    pairs = blocks // scales.shape[0]
    order_copy = pltpu.make_async_copy(order_in.at[0], order, sem.at[0])
    order_copy.start()
    stores = [
        pltpu.make_async_copy(left, new_left, sem.at[1]),
        pltpu.make_async_copy(right, new_right, sem.at[2]),
    ]
    for store in stores:
        store.start()
    order_copy.wait()

    def give(there, carry):
        for p in range(pairs):
            s = pairs * there + p
            arranged[order[s]] = (tiles[s].astype(F32) * scales[there, p : p + 1]).astype(BF16)
        return carry

    lax.fori_loop(0, scales.shape[0], give, 0, unroll=2)
    last = pltpu.make_async_copy(arranged, update, sem.at[3])
    last.start()
    last.wait()
    for store in stores:
        store.wait()


def body(nd, nm, grads, order, left_stat, right_stat, left_root, right_root):
    blocks, rows, cols = grads.shape
    _, half, width = left_stat.shape
    vmem = pl.BlockSpec(memory_space=pltpu.VMEM)
    half_shape = left_stat.shape
    hbm = pl.BlockSpec(memory_space=pltpu.HBM)
    dma = pltpu.SemaphoreType.DMA
    operands = [order.reshape(1, blocks), grads, left_stat, right_stat, left_root, right_root]
    operands = [pltpu.with_memory_space_constraint(x, pltpu.HBM) for x in operands]
    products = 4 * half * width * width
    results = pl.pallas_call(
        functools.partial(kernel, nd, nm),
        out_shape=(
            pltpu.VMEM(left_stat.shape, F32),
            pltpu.VMEM(right_stat.shape, F32),
            pltpu.VMEM(grads.shape, BF16),
            pltpu.VMEM((nd, 8, 128), F32),
        ),
        in_specs=[hbm] * 6,
        out_specs=(vmem, vmem, vmem, vmem),
        scratch_shapes=[
            pltpu.SMEM((blocks,), jnp.int32),
            pltpu.VMEM((blocks, rows, cols), BF16),
            pltpu.VMEM((blocks, rows, cols), BF16),
            pltpu.VMEM((nm, width, cols), BF16),
            pltpu.VMEM((width, width), BF16),
            pltpu.VMEM((half, width), BF16),
            pltpu.VMEM((width, width), BF16),
            pltpu.VMEM((half, width), F32),
            pltpu.VMEM((half, cols), BF16),
            pltpu.VMEM((nm, half, cols), BF16),
            pltpu.VMEM((half, cols), BF16),
            pltpu.VMEM((nd, 8, 128), F32),
            pltpu.VMEM((8, 128), F32),
            pltpu.VMEM((nm, 8, 128), F32),
            pltpu.VMEM((8, 128), F32),
            pltpu.VMEM((nm, 8, 128), F32),
            dma((6,)),
            dma((nm,)),
            dma,
            dma((nm,)),
            dma((2,)),
            dma((2,)),
            dma((2,)),
            dma((2,)),
            dma((2,)),
            dma,
            dma,
            dma((2,)),
            pltpu.SemaphoreType.REGULAR,
        ],
        compiler_params=pltpu.CompilerParams(
            collective_id=0, has_side_effects=True, vmem_limit_bytes=48 * 1024 * 1024
        ),
        cost_estimate=pl.CostEstimate(
            flops=2 * products, bytes_accessed=12 * half * width * 2, transcendentals=0
        ),
        name="step",
    )(*operands)
    return pl.pallas_call(
        finish_kernel,
        out_shape=(
            pltpu.HBM(half_shape, F32),
            pltpu.HBM(half_shape, F32),
            pltpu.HBM(grads.shape, BF16),
        ),
        in_specs=[hbm, vmem, vmem, vmem, vmem],
        out_specs=(hbm, hbm, hbm),
        scratch_shapes=[
            pltpu.SMEM((blocks,), jnp.int32),
            pltpu.VMEM(grads.shape, BF16),
            dma((4,)),
        ],
        compiler_params=pltpu.CompilerParams(vmem_limit_bytes=8 * 1024 * 1024),
        cost_estimate=pl.CostEstimate(flops=0, bytes_accessed=10 * half * width, transcendentals=0),
        name="finish",
    )(operands[0], *results)


def solution(mesh):
    owned = P(("dp", "mp"), None, None)
    return jax.shard_map(
        functools.partial(body, mesh.shape["dp"], mesh.shape["mp"]),
        mesh=mesh,
        in_specs=(P(None, "dp", "mp"), P(), owned, owned, owned, owned),
        out_specs=(owned, owned, P(None, "dp", "mp")),
        check_vma=False,
    )
```

```python
import functools

import jax
import jax.numpy as jnp
from jax import lax
from jax.experimental import pallas as pl
from jax.experimental.pallas import tpu as pltpu
from jax.sharding import PartitionSpec as P

MESH = pl.DeviceIdType.MESH
F32 = jnp.float32
BF16 = jnp.bfloat16
beta_two = 0.95
clip_rms = 0.5


def fold(x):
    x = x.astype(F32)
    return jnp.sum((x * x).reshape(-1, 8, 128), axis=0)


def everything(x):
    return jnp.sum(jnp.sum(x, axis=0, keepdims=True), axis=1, keepdims=True)


def kernel(
    nd,
    nm,
    order_in,
    grads_in,
    left_stat,
    right_stat,
    left_root,
    right_root,
    new_left,
    new_right,
    u_in,
    scales,
    order,
    grads,
    tiles,
    slabs,
    full,
    lroot,
    rroot,
    acc,
    last_a,
    u_out,
    relay,
    sq_dp,
    sq_mine,
    sq_mp,
    g_sq,
    sums,
    load_sem,
    slab_sem,
    tile_sem,
    forward_sem,
    root_sem,
    sq_send_sem,
    sq_recv_sem,
    sum_send_sem,
    sum_recv_sem,
    u_send_sem,
    u_recv_sem,
    relay_sem,
    ready_sem,
):
    blocks, rows, cols = grads.shape
    half, width = lroot.shape
    pairs = nm // 2
    d = lax.axis_index("dp")
    m = lax.axis_index("mp")
    h = m % 2
    pair = m // 2
    sigma = 2 * h - 1
    partner = m - sigma
    per_half = nd // 2
    my_rows = pl.ds(pl.multiple_of(h * half, half), half)

    def place(offset):
        return (m + offset + 2 * nm) % nm

    first_loads = [
        pltpu.make_async_copy(order_in.at[0], order, load_sem.at[4]),
        pltpu.make_async_copy(grads_in, grads, load_sem.at[5]),
    ]
    for load in first_loads:
        load.start()

    barrier = pltpu.get_barrier_semaphore()

    def greet(k, carry):
        pl.semaphore_signal(barrier, inc=1, device_id=((d + k) % nd, m), device_id_type=MESH)
        return carry

    lax.fori_loop(1, nd, greet, 0)
    for k in range(1, nm):
        pl.semaphore_signal(barrier, inc=1, device_id=(d, (m + k) % nm), device_id_type=MESH)

    loads = [
        pltpu.make_async_copy(left_root.at[0], lroot, load_sem.at[0]),
        pltpu.make_async_copy(right_root.at[0], rroot.at[my_rows], load_sem.at[1]),
        pltpu.make_async_copy(left_stat, new_left, load_sem.at[2]),
        pltpu.make_async_copy(right_stat, new_right, load_sem.at[3]),
    ]

    pl.semaphore_wait(barrier, nd - 1 + nm - 1)
    for k in range(1, nm):
        pl.semaphore_signal(ready_sem, inc=1, device_id=(d, (m + k) % nm), device_id_type=MESH)

    part_rows = half // 4

    def root_copy(n):
        return pltpu.make_async_remote_copy(
            src_ref=right_root.at[0, pl.ds(n * part_rows, part_rows)],
            dst_ref=rroot.at[pl.ds(pl.multiple_of(h * half + n * part_rows, part_rows), part_rows)],
            send_sem=root_sem.at[0],
            recv_sem=root_sem.at[1],
            device_id=(d, partner),
            device_id_type=MESH,
        )

    root_copy(0).start()
    for load in loads:
        load.start()

    targets = [place(3 * sigma), place(-2 * sigma), place(sigma), m]

    groups = min(4, nd)
    group_places = nd // groups
    group_rows = width // groups
    group = d // group_places

    def tile_copy(there, target):
        return pltpu.make_async_remote_copy(
            src_ref=tiles.at[pairs * there + target // 2],
            dst_ref=slabs.at[m, pl.ds(pl.multiple_of(d * rows, rows), rows)],
            send_sem=tile_sem,
            recv_sem=slab_sem.at[m, group],
            device_id=(there, target),
            device_id_type=MESH,
        )

    def arrange(there, total):
        for p in range(pairs):
            s = pairs * there + p
            tile = grads[order[s]]
            tiles[s] = tile
            total = total + fold(tile)
        return total

    for load in first_loads:
        load.wait()
    pl.semaphore_wait(ready_sem, nm - 1)
    total = arrange(d, jnp.zeros((8, 128), F32))
    for target in targets[:3]:
        tile_copy(d, target).start()
    pltpu.make_async_copy(
        tiles.at[pairs * d + pair],
        slabs.at[m, pl.ds(pl.multiple_of(d * rows, rows), rows)],
        slab_sem.at[m, group],
    ).start()

    def send_tiles(k, total):
        there_group = (group - k // group_places + groups) % groups
        there = there_group * group_places + (d + 3 * k) % group_places
        total = arrange(there, total)
        for target in targets:
            tile_copy(there, target).start()
        return total

    sq_dp[d] = lax.fori_loop(1, nd, send_tiles, total)

    for n in range(1, 4):
        root_copy(n).start()

    def send_sq(k, carry):
        pltpu.make_async_remote_copy(
            src_ref=sq_dp.at[d],
            dst_ref=sq_dp.at[d],
            send_sem=sq_send_sem.at[0],
            recv_sem=sq_recv_sem.at[0],
            device_id=((d + k) % nd, m),
            device_id_type=MESH,
        ).start()
        return carry

    lax.fori_loop(1, nd, send_sq, 0)
    some = sq_dp.at[pl.ds(0, nd - 1)]
    pltpu.make_async_copy(some, some, sq_recv_sem.at[0]).wait()
    sq_mine[...] = jnp.sum(sq_dp[...], axis=0)
    sq_mp[m] = sq_mine[...]
    for k in range(1, nm):
        pltpu.make_async_remote_copy(
            src_ref=sq_mine,
            dst_ref=sq_mp.at[m],
            send_sem=sq_send_sem.at[1],
            recv_sem=sq_recv_sem.at[1],
            device_id=(d, (m + k) % nm),
            device_id_type=MESH,
        ).start()

    def part_of(k, g):
        return slabs.at[k, pl.ds(pl.multiple_of(g * group_rows, group_rows), group_rows)]

    def wait_part(k, g):
        pltpu.make_async_copy(part_of(k, g), part_of(k, g), slab_sem.at[k, g]).wait()

    def wait_slab(k):
        for g in range(groups):
            wait_part(k, g)

    def forward(c, carry):
        g = (group + c) % groups
        for j in range(pairs):
            k = place(j * sigma)
            wait_part(k, g)
            pltpu.make_async_remote_copy(
                src_ref=part_of(k, g),
                dst_ref=part_of(k, g),
                send_sem=forward_sem,
                recv_sem=slab_sem.at[k, g],
                device_id=(d, partner),
                device_id_type=MESH,
            ).start()
        return carry

    lax.fori_loop(0, groups, forward, 0)

    loads[0].wait()
    loads[1].wait()
    pltpu.make_async_copy(lroot, lroot, root_sem.at[1]).wait()
    acc[...] = jnp.zeros_like(acc)
    g_sq[...] = jnp.zeros_like(g_sq)

    def through_left(k):
        slab = slabs[k]
        g_sq[...] += fold(slab)
        return jnp.dot(lroot[...], slab, preferred_element_type=F32).astype(BF16)

    def right_rows(k):
        return pl.ds(pl.multiple_of(k * cols, cols), cols)

    def use_slab(k):
        a = through_left(k)
        acc[...] += jnp.dot(a, rroot[right_rows(k)], preferred_element_type=F32)

    def near(j, carry):
        use_slab(place(j * sigma))
        return carry

    def far(j, carry):
        k = place(-(j + 1) * sigma)
        wait_slab(k)
        use_slab(k)
        return carry

    lax.fori_loop(0, pairs, near, 0)
    lax.fori_loop(0, pairs - 1, far, 0)
    last = place(-pairs * sigma)
    wait_slab(last)
    last_a[...] = through_left(last)
    step = 2 * cols

    opposite = place(nm // 2)

    def finish(i, total):
        n = (opposite // 2 + i) % pairs
        part = pl.ds(pl.multiple_of(n * step, step), step)
        u = acc[:, part] + jnp.dot(
            last_a[...], rroot[right_rows(last), part], preferred_element_type=F32
        )
        u_out[2 * n] = u[:, :cols].astype(BF16)
        u_out[2 * n + 1] = u[:, cols:].astype(BF16)
        return total + fold(u[:, :cols]) + fold(u[:, cols:])

    slot = pairs * d + pair

    def u_copy(near_row, target):
        return pltpu.make_async_remote_copy(
            src_ref=u_out.at[target, pl.ds(pl.multiple_of(near_row * rows, rows), rows)],
            dst_ref=u_in.at[slot],
            send_sem=u_send_sem,
            recv_sem=u_recv_sem,
            device_id=(h * per_half + near_row, target),
            device_id_type=MESH,
        )

    u_sq = finish(0, jnp.zeros((8, 128), F32))
    relay_copy = pltpu.make_async_remote_copy(
        src_ref=u_out.at[opposite],
        dst_ref=relay,
        send_sem=relay_sem.at[0],
        recv_sem=relay_sem.at[1],
        device_id=(d, partner),
        device_id_type=MESH,
    )
    relay_copy.start()
    beside = place(3 * sigma)

    def send_beside(k, carry):
        u_copy((d + 7 * k) % per_half, beside).start()
        return carry

    lax.fori_loop(0, per_half, send_beside, 0)
    u_sq = lax.fori_loop(1, pairs, finish, u_sq)

    row = lax.broadcasted_iota(jnp.int32, (8, 128), 0)
    sums[m] = jnp.where(row < 4, everything(u_sq), everything(g_sq[...]))
    for k in range(1, nm):
        pltpu.make_async_remote_copy(
            src_ref=sums.at[m],
            dst_ref=sums.at[m],
            send_sem=sum_send_sem.at[0],
            recv_sem=sum_recv_sem.at[0],
            device_id=(d, (m + k) % nm),
            device_id_type=MESH,
        ).start()

    own_half = d // per_half == h

    def send_u(k, carry):
        near_row = (d + 7 * k) % per_half
        for j in (-3, 2, -2, 1, -1):
            u_copy(near_row, place(j * sigma)).start()
        here = jnp.logical_and(own_half, k == 0)

        @pl.when(here)
        def _():
            pltpu.make_async_copy(
                u_out.at[m, pl.ds(pl.multiple_of(near_row * rows, rows), rows)],
                u_in.at[slot],
                u_recv_sem,
            ).start()

        @pl.when(jnp.logical_not(here))
        def _():
            u_copy(near_row, m).start()

        return carry

    lax.fori_loop(0, per_half // 2, send_u, 0)
    relay_copy.wait_recv()

    def pass_on(k, carry):
        near_row = (d + 7 * k) % per_half
        pltpu.make_async_remote_copy(
            src_ref=relay.at[pl.ds(pl.multiple_of(near_row * rows, rows), rows)],
            dst_ref=u_in.at[slot],
            send_sem=u_send_sem,
            recv_sem=u_recv_sem,
            device_id=((1 - h) * per_half + near_row, (partner + nm // 2) % nm),
            device_id_type=MESH,
        ).start()
        return carry

    lax.fori_loop(0, per_half, pass_on, 0)

    some_mp = sq_mp.at[pl.ds(0, nm - 1)]
    pltpu.make_async_copy(some_mp, some_mp, sq_recv_sem.at[1]).wait()
    total_sq = everything(jnp.sum(sq_mp[...], axis=0))
    clip = jnp.minimum(1.0, clip_rms * jnp.sqrt(F32(blocks * width * width)) / jnp.sqrt(total_sq + 1e-06))
    coefficient = (1.0 - beta_two) * clip * clip
    pltpu.make_async_copy(some_mp, some_mp, sum_recv_sem.at[0]).wait()
    mine = jnp.zeros((8, 128), F32)
    for p in range(pairs):
        u_total = sums[2 * p, 0:1] + sums[2 * p + 1, 0:1]
        scale = -(clip * jnp.sqrt(sums[2 * p, 4:5]) / jnp.sqrt(u_total + 1e-06))
        mine = jnp.where(row == p, scale, mine)
    scales[d] = mine

    def send_scales(k, carry):
        pltpu.make_async_remote_copy(
            src_ref=scales.at[d],
            dst_ref=scales.at[d],
            send_sem=sum_send_sem.at[1],
            recv_sem=sum_recv_sem.at[1],
            device_id=((d + k) % nd, m),
            device_id_type=MESH,
        ).start()
        return carry

    lax.fori_loop(1, nd, send_scales, 0)
    lax.fori_loop(per_half // 2, per_half, send_u, 0)

    for k in range(nm):
        full[:, k * cols : (k + 1) * cols] = slabs[k]
    loads[2].wait()

    def left_gram(n, carry):
        part = pl.ds(pl.multiple_of(n * step, step), step)
        gram = lax.dot_general(
            full[my_rows], full[part], (((1,), (1,)), ((), ())), preferred_element_type=F32
        )
        new_left[0, :, part] = beta_two * new_left[0, :, part] + coefficient * gram
        return carry

    lax.fori_loop(0, width // step, left_gram, 0)
    loads[3].wait()

    def right_gram(n, carry):
        part = pl.ds(pl.multiple_of(n * step, step), step)
        gram = lax.dot_general(
            full[:, my_rows], full[:, part], (((0,), (0,)), ((), ())), preferred_element_type=F32
        )
        new_right[0, :, part] = beta_two * new_right[0, :, part] + coefficient * gram
        return carry

    lax.fori_loop(0, width // step, right_gram, 0)

    sent = tiles.at[pl.ds(0, blocks - 1)]
    pltpu.make_async_copy(sent, sent, tile_sem).wait()
    pltpu.make_async_copy(lroot, lroot, root_sem.at[0]).wait()
    pltpu.make_async_copy(some, some, sq_send_sem.at[0]).wait()
    pltpu.make_async_copy(some_mp, some_mp, sq_send_sem.at[1]).wait()
    pltpu.make_async_copy(some_mp, some_mp, sum_send_sem.at[0]).wait()
    pltpu.make_async_copy(some, some, sum_send_sem.at[1]).wait()
    relay_copy.wait_send()
    pltpu.make_async_copy(lroot, lroot, forward_sem).wait()

    @pl.when(own_half)
    def _():
        pltpu.make_async_copy(sent, sent, u_send_sem).wait()

    @pl.when(jnp.logical_not(own_half))
    def _():
        pltpu.make_async_copy(tiles, tiles, u_send_sem).wait()

    pltpu.make_async_copy(some, some, sum_recv_sem.at[1]).wait()
    pltpu.make_async_copy(u_in, u_in, u_recv_sem).wait()


def finish_kernel(order_in, left, right, tiles, scales, new_left, new_right, update, order, arranged, sem):
    blocks = tiles.shape[0]
    pairs = blocks // scales.shape[0]
    order_copy = pltpu.make_async_copy(order_in.at[0], order, sem.at[0])
    order_copy.start()
    stores = [
        pltpu.make_async_copy(left, new_left, sem.at[1]),
        pltpu.make_async_copy(right, new_right, sem.at[2]),
    ]
    for store in stores:
        store.start()
    order_copy.wait()

    def give(there, carry):
        for p in range(pairs):
            s = pairs * there + p
            arranged[order[s]] = (tiles[s].astype(F32) * scales[there, p : p + 1]).astype(BF16)
        return carry

    lax.fori_loop(0, scales.shape[0], give, 0, unroll=2)
    last = pltpu.make_async_copy(arranged, update, sem.at[3])
    last.start()
    last.wait()
    for store in stores:
        store.wait()


def body(nd, nm, grads, order, left_stat, right_stat, left_root, right_root):
    blocks, rows, cols = grads.shape
    _, half, width = left_stat.shape
    vmem = pl.BlockSpec(memory_space=pltpu.VMEM)
    half_shape = left_stat.shape
    hbm = pl.BlockSpec(memory_space=pltpu.HBM)
    dma = pltpu.SemaphoreType.DMA
    operands = [order.reshape(1, blocks), grads, left_stat, right_stat, left_root, right_root]
    operands = [pltpu.with_memory_space_constraint(x, pltpu.HBM) for x in operands]
    products = 4 * half * width * width
    results = pl.pallas_call(
        functools.partial(kernel, nd, nm),
        out_shape=(
            pltpu.VMEM(left_stat.shape, F32),
            pltpu.VMEM(right_stat.shape, F32),
            pltpu.VMEM(grads.shape, BF16),
            pltpu.VMEM((nd, 8, 128), F32),
        ),
        in_specs=[hbm] * 6,
        out_specs=(vmem, vmem, vmem, vmem),
        scratch_shapes=[
            pltpu.SMEM((blocks,), jnp.int32),
            pltpu.VMEM((blocks, rows, cols), BF16),
            pltpu.VMEM((blocks, rows, cols), BF16),
            pltpu.VMEM((nm, width, cols), BF16),
            pltpu.VMEM((width, width), BF16),
            pltpu.VMEM((half, width), BF16),
            pltpu.VMEM((width, width), BF16),
            pltpu.VMEM((half, width), F32),
            pltpu.VMEM((half, cols), BF16),
            pltpu.VMEM((nm, half, cols), BF16),
            pltpu.VMEM((half, cols), BF16),
            pltpu.VMEM((nd, 8, 128), F32),
            pltpu.VMEM((8, 128), F32),
            pltpu.VMEM((nm, 8, 128), F32),
            pltpu.VMEM((8, 128), F32),
            pltpu.VMEM((nm, 8, 128), F32),
            dma((6,)),
            dma((nm, 4)),
            dma,
            dma,
            dma((2,)),
            dma((2,)),
            dma((2,)),
            dma((2,)),
            dma((2,)),
            dma,
            dma,
            dma((2,)),
            pltpu.SemaphoreType.REGULAR,
        ],
        compiler_params=pltpu.CompilerParams(
            collective_id=0, has_side_effects=True, vmem_limit_bytes=48 * 1024 * 1024
        ),
        cost_estimate=pl.CostEstimate(
            flops=2 * products, bytes_accessed=12 * half * width * 2, transcendentals=0
        ),
        name="step",
    )(*operands)
    return pl.pallas_call(
        finish_kernel,
        out_shape=(
            pltpu.HBM(half_shape, F32),
            pltpu.HBM(half_shape, F32),
            pltpu.HBM(grads.shape, BF16),
        ),
        in_specs=[hbm, vmem, vmem, vmem, vmem],
        out_specs=(hbm, hbm, hbm),
        scratch_shapes=[
            pltpu.SMEM((blocks,), jnp.int32),
            pltpu.VMEM(grads.shape, BF16),
            dma((4,)),
        ],
        compiler_params=pltpu.CompilerParams(vmem_limit_bytes=8 * 1024 * 1024),
        cost_estimate=pl.CostEstimate(flops=0, bytes_accessed=10 * half * width, transcendentals=0),
        name="finish",
    )(operands[0], *results)


def solution(mesh):
    owned = P(("dp", "mp"), None, None)
    return jax.shard_map(
        functools.partial(body, mesh.shape["dp"], mesh.shape["mp"]),
        mesh=mesh,
        in_specs=(P(None, "dp", "mp"), P(), owned, owned, owned, owned),
        out_specs=(owned, owned, P(None, "dp", "mp")),
        check_vma=False,
    )
```

```python
import functools

import jax
import jax.numpy as jnp
from jax import lax
from jax.experimental import pallas as pl
from jax.experimental.pallas import tpu as pltpu
from jax.sharding import PartitionSpec as P

MESH = pl.DeviceIdType.MESH
F32 = jnp.float32
BF16 = jnp.bfloat16
beta_two = 0.95
clip_rms = 0.5


def fold(x):
    x = x.astype(F32)
    return jnp.sum((x * x).reshape(-1, 8, 128), axis=0)


def everything(x):
    return jnp.sum(jnp.sum(x, axis=0, keepdims=True), axis=1, keepdims=True)


def kernel(
    nd,
    nm,
    order_in,
    grads_in,
    left_stat,
    right_stat,
    left_root,
    right_root,
    new_left,
    new_right,
    u_in,
    scales,
    inverse,
    order,
    order_row,
    grads,
    tiles,
    slabs,
    full,
    lroot,
    rroot,
    acc,
    last_a,
    u_out,
    relay,
    sq_dp,
    sq_mine,
    sq_mp,
    g_sq,
    sums,
    load_sem,
    slab_sem,
    tile_sem,
    forward_sem,
    root_sem,
    sq_send_sem,
    sq_recv_sem,
    sum_send_sem,
    sum_recv_sem,
    u_send_sem,
    u_recv_sem,
    relay_sem,
    ready_sem,
):
    blocks, rows, cols = grads.shape
    half, width = lroot.shape
    pairs = nm // 2
    d = lax.axis_index("dp")
    m = lax.axis_index("mp")
    h = m % 2
    pair = m // 2
    sigma = 2 * h - 1
    partner = m - sigma
    per_half = nd // 2
    my_rows = pl.ds(pl.multiple_of(h * half, half), half)

    def place(offset):
        return (m + offset + 2 * nm) % nm

    first_loads = [
        pltpu.make_async_copy(order_in.at[0], order, load_sem.at[4]),
        pltpu.make_async_copy(grads_in, grads, load_sem.at[5]),
        pltpu.make_async_copy(order_in, order_row, load_sem.at[6]),
    ]
    for load in first_loads:
        load.start()

    barrier = pltpu.get_barrier_semaphore()

    def greet(k, carry):
        pl.semaphore_signal(barrier, inc=1, device_id=((d + k) % nd, m), device_id_type=MESH)
        return carry

    lax.fori_loop(1, nd, greet, 0)
    for k in range(1, nm):
        pl.semaphore_signal(barrier, inc=1, device_id=(d, (m + k) % nm), device_id_type=MESH)

    loads = [
        pltpu.make_async_copy(left_root.at[0], lroot, load_sem.at[0]),
        pltpu.make_async_copy(right_root.at[0], rroot.at[my_rows], load_sem.at[1]),
        pltpu.make_async_copy(left_stat, new_left, load_sem.at[2]),
        pltpu.make_async_copy(right_stat, new_right, load_sem.at[3]),
    ]

    pl.semaphore_wait(barrier, nd - 1 + nm - 1)
    for k in range(1, nm):
        pl.semaphore_signal(ready_sem, inc=1, device_id=(d, (m + k) % nm), device_id_type=MESH)

    part_rows = half // 4

    def root_copy(n):
        return pltpu.make_async_remote_copy(
            src_ref=right_root.at[0, pl.ds(n * part_rows, part_rows)],
            dst_ref=rroot.at[pl.ds(pl.multiple_of(h * half + n * part_rows, part_rows), part_rows)],
            send_sem=root_sem.at[0],
            recv_sem=root_sem.at[1],
            device_id=(d, partner),
            device_id_type=MESH,
        )

    root_copy(0).start()
    for load in loads:
        load.start()

    targets = [place(3 * sigma), place(-2 * sigma), place(sigma), m]

    groups = min(4, nd)
    group_places = nd // groups
    group_rows = width // groups
    group = d // group_places

    def tile_copy(there, target):
        return pltpu.make_async_remote_copy(
            src_ref=tiles.at[pairs * there + target // 2],
            dst_ref=slabs.at[m, pl.ds(pl.multiple_of(d * rows, rows), rows)],
            send_sem=tile_sem,
            recv_sem=slab_sem.at[m, group],
            device_id=(there, target),
            device_id_type=MESH,
        )

    def arrange(there, total):
        for p in range(pairs):
            s = pairs * there + p
            tile = grads[order[s]]
            tiles[s] = tile
            total = total + fold(tile)
        return total

    for load in first_loads:
        load.wait()
    pl.semaphore_wait(ready_sem, nm - 1)
    total = arrange(d, jnp.zeros((8, 128), F32))
    for target in targets[:3]:
        tile_copy(d, target).start()
    pltpu.make_async_copy(
        tiles.at[pairs * d + pair],
        slabs.at[m, pl.ds(pl.multiple_of(d * rows, rows), rows)],
        slab_sem.at[m, group],
    ).start()

    def send_tiles(k, total):
        there_group = (group - k // group_places + groups) % groups
        there = there_group * group_places + (d + 3 * k) % group_places
        total = arrange(there, total)
        for target in targets:
            tile_copy(there, target).start()
        return total

    sq_dp[d] = lax.fori_loop(1, nd, send_tiles, total)

    for n in range(1, 4):
        root_copy(n).start()

    def send_sq(k, carry):
        pltpu.make_async_remote_copy(
            src_ref=sq_dp.at[d],
            dst_ref=sq_dp.at[d],
            send_sem=sq_send_sem.at[0],
            recv_sem=sq_recv_sem.at[0],
            device_id=((d + k) % nd, m),
            device_id_type=MESH,
        ).start()
        return carry

    lax.fori_loop(1, nd, send_sq, 0)
    some = sq_dp.at[pl.ds(0, nd - 1)]
    pltpu.make_async_copy(some, some, sq_recv_sem.at[0]).wait()
    sq_mine[...] = jnp.sum(sq_dp[...], axis=0)
    sq_mp[m] = sq_mine[...]
    for k in range(1, nm):
        pltpu.make_async_remote_copy(
            src_ref=sq_mine,
            dst_ref=sq_mp.at[m],
            send_sem=sq_send_sem.at[1],
            recv_sem=sq_recv_sem.at[1],
            device_id=(d, (m + k) % nm),
            device_id_type=MESH,
        ).start()

    def part_of(k, g):
        return slabs.at[k, pl.ds(pl.multiple_of(g * group_rows, group_rows), group_rows)]

    def wait_part(k, g):
        pltpu.make_async_copy(part_of(k, g), part_of(k, g), slab_sem.at[k, g]).wait()

    def wait_slab(k):
        for g in range(groups):
            wait_part(k, g)

    def forward(c, carry):
        g = (group + c) % groups
        for j in range(pairs):
            k = place(j * sigma)
            wait_part(k, g)
            pltpu.make_async_remote_copy(
                src_ref=part_of(k, g),
                dst_ref=part_of(k, g),
                send_sem=forward_sem,
                recv_sem=slab_sem.at[k, g],
                device_id=(d, partner),
                device_id_type=MESH,
            ).start()
        return carry

    lax.fori_loop(0, groups, forward, 0)

    spread = jnp.transpose(jnp.broadcast_to(order_row[...], (blocks, blocks)))
    slot_of = lax.broadcasted_iota(jnp.int32, (blocks, blocks), 0)
    block_of = lax.broadcasted_iota(jnp.int32, (blocks, blocks), 1)
    inverse[...] = jnp.max(jnp.where(spread == block_of, slot_of, 0), axis=0, keepdims=True)

    loads[0].wait()
    loads[1].wait()
    pltpu.make_async_copy(lroot, lroot, root_sem.at[1]).wait()
    acc[...] = jnp.zeros_like(acc)
    g_sq[...] = jnp.zeros_like(g_sq)

    def through_left(k):
        slab = slabs[k]
        g_sq[...] += fold(slab)
        return jnp.dot(lroot[...], slab, preferred_element_type=F32).astype(BF16)

    def right_rows(k):
        return pl.ds(pl.multiple_of(k * cols, cols), cols)

    def use_slab(k):
        a = through_left(k)
        acc[...] += jnp.dot(a, rroot[right_rows(k)], preferred_element_type=F32)

    def near(j, carry):
        use_slab(place(j * sigma))
        return carry

    def far(j, carry):
        k = place(-(j + 1) * sigma)
        wait_slab(k)
        use_slab(k)
        return carry

    lax.fori_loop(0, pairs, near, 0)
    lax.fori_loop(0, pairs - 1, far, 0)
    last = place(-pairs * sigma)
    wait_slab(last)
    last_a[...] = through_left(last)
    step = 2 * cols

    opposite = place(nm // 2)

    def finish(i, total):
        n = (opposite // 2 + i) % pairs
        part = pl.ds(pl.multiple_of(n * step, step), step)
        u = acc[:, part] + jnp.dot(
            last_a[...], rroot[right_rows(last), part], preferred_element_type=F32
        )
        u_out[2 * n] = u[:, :cols].astype(BF16)
        u_out[2 * n + 1] = u[:, cols:].astype(BF16)
        return total + fold(u[:, :cols]) + fold(u[:, cols:])

    slot = pairs * d + pair

    def u_copy(near_row, target):
        return pltpu.make_async_remote_copy(
            src_ref=u_out.at[target, pl.ds(pl.multiple_of(near_row * rows, rows), rows)],
            dst_ref=u_in.at[slot],
            send_sem=u_send_sem,
            recv_sem=u_recv_sem,
            device_id=(h * per_half + near_row, target),
            device_id_type=MESH,
        )

    u_sq = finish(0, jnp.zeros((8, 128), F32))
    relay_copy = pltpu.make_async_remote_copy(
        src_ref=u_out.at[opposite],
        dst_ref=relay,
        send_sem=relay_sem.at[0],
        recv_sem=relay_sem.at[1],
        device_id=(d, partner),
        device_id_type=MESH,
    )
    relay_copy.start()
    beside = place(3 * sigma)

    def send_beside(k, carry):
        u_copy((d + 7 * k) % per_half, beside).start()
        return carry

    lax.fori_loop(0, per_half, send_beside, 0)
    u_sq = lax.fori_loop(1, pairs, finish, u_sq)

    row = lax.broadcasted_iota(jnp.int32, (8, 128), 0)
    sums[m] = jnp.where(row < 4, everything(u_sq), everything(g_sq[...]))
    for k in range(1, nm):
        pltpu.make_async_remote_copy(
            src_ref=sums.at[m],
            dst_ref=sums.at[m],
            send_sem=sum_send_sem.at[0],
            recv_sem=sum_recv_sem.at[0],
            device_id=(d, (m + k) % nm),
            device_id_type=MESH,
        ).start()

    own_half = d // per_half == h

    def send_u(k, carry):
        near_row = (d + 7 * k) % per_half
        for j in (-3, 2, -2, 1, -1):
            u_copy(near_row, place(j * sigma)).start()
        here = jnp.logical_and(own_half, k == 0)

        @pl.when(here)
        def _():
            pltpu.make_async_copy(
                u_out.at[m, pl.ds(pl.multiple_of(near_row * rows, rows), rows)],
                u_in.at[slot],
                u_recv_sem,
            ).start()

        @pl.when(jnp.logical_not(here))
        def _():
            u_copy(near_row, m).start()

        return carry

    lax.fori_loop(0, per_half // 2, send_u, 0)
    relay_copy.wait_recv()

    def pass_on(k, carry):
        near_row = (d + 7 * k) % per_half
        pltpu.make_async_remote_copy(
            src_ref=relay.at[pl.ds(pl.multiple_of(near_row * rows, rows), rows)],
            dst_ref=u_in.at[slot],
            send_sem=u_send_sem,
            recv_sem=u_recv_sem,
            device_id=((1 - h) * per_half + near_row, (partner + nm // 2) % nm),
            device_id_type=MESH,
        ).start()
        return carry

    lax.fori_loop(0, per_half, pass_on, 0)

    some_mp = sq_mp.at[pl.ds(0, nm - 1)]
    pltpu.make_async_copy(some_mp, some_mp, sq_recv_sem.at[1]).wait()
    total_sq = everything(jnp.sum(sq_mp[...], axis=0))
    clip = jnp.minimum(1.0, clip_rms * jnp.sqrt(F32(blocks * width * width)) / jnp.sqrt(total_sq + 1e-06))
    coefficient = (1.0 - beta_two) * clip * clip
    pltpu.make_async_copy(some_mp, some_mp, sum_recv_sem.at[0]).wait()
    mine = jnp.zeros((8, 128), F32)
    for p in range(pairs):
        u_total = sums[2 * p, 0:1] + sums[2 * p + 1, 0:1]
        scale = -(clip * jnp.sqrt(sums[2 * p, 4:5]) / jnp.sqrt(u_total + 1e-06))
        mine = jnp.where(row == p, scale, mine)
    scales[d] = mine

    def send_scales(k, carry):
        pltpu.make_async_remote_copy(
            src_ref=scales.at[d],
            dst_ref=scales.at[d],
            send_sem=sum_send_sem.at[1],
            recv_sem=sum_recv_sem.at[1],
            device_id=((d + k) % nd, m),
            device_id_type=MESH,
        ).start()
        return carry

    lax.fori_loop(1, nd, send_scales, 0)
    lax.fori_loop(per_half // 2, per_half, send_u, 0)

    for k in range(nm):
        full[:, k * cols : (k + 1) * cols] = slabs[k]
    loads[2].wait()

    def left_gram(n, carry):
        part = pl.ds(pl.multiple_of(n * step, step), step)
        gram = lax.dot_general(
            full[my_rows], full[part], (((1,), (1,)), ((), ())), preferred_element_type=F32
        )
        new_left[0, :, part] = beta_two * new_left[0, :, part] + coefficient * gram
        return carry

    lax.fori_loop(0, width // step, left_gram, 0)
    loads[3].wait()

    def right_gram(n, carry):
        part = pl.ds(pl.multiple_of(n * step, step), step)
        gram = lax.dot_general(
            full[:, my_rows], full[:, part], (((0,), (0,)), ((), ())), preferred_element_type=F32
        )
        new_right[0, :, part] = beta_two * new_right[0, :, part] + coefficient * gram
        return carry

    lax.fori_loop(0, width // step, right_gram, 0)

    sent = tiles.at[pl.ds(0, blocks - 1)]
    pltpu.make_async_copy(sent, sent, tile_sem).wait()
    pltpu.make_async_copy(lroot, lroot, root_sem.at[0]).wait()
    pltpu.make_async_copy(some, some, sq_send_sem.at[0]).wait()
    pltpu.make_async_copy(some_mp, some_mp, sq_send_sem.at[1]).wait()
    pltpu.make_async_copy(some_mp, some_mp, sum_send_sem.at[0]).wait()
    pltpu.make_async_copy(some, some, sum_send_sem.at[1]).wait()
    relay_copy.wait_send()
    pltpu.make_async_copy(lroot, lroot, forward_sem).wait()

    @pl.when(own_half)
    def _():
        pltpu.make_async_copy(sent, sent, u_send_sem).wait()

    @pl.when(jnp.logical_not(own_half))
    def _():
        pltpu.make_async_copy(tiles, tiles, u_send_sem).wait()

    pltpu.make_async_copy(some, some, sum_recv_sem.at[1]).wait()
    pltpu.make_async_copy(u_in, u_in, u_recv_sem).wait()


def finish_kernel(
    left, right, tiles, scales, inverse_in, new_left, new_right, update, inverse, scaled, arranged, sem
):
    places = scales.shape[0]
    blocks = tiles.shape[0]
    pairs = blocks // places
    inverse_copy = pltpu.make_async_copy(inverse_in.at[0], inverse, sem.at[0])
    inverse_copy.start()
    stores = [
        pltpu.make_async_copy(left, new_left, sem.at[1]),
        pltpu.make_async_copy(right, new_right, sem.at[2]),
    ]
    for store in stores:
        store.start()

    def scale(there, carry):
        for p in range(pairs):
            s = pairs * there + p
            scaled[s] = (tiles[s].astype(F32) * scales[there, p : p + 1]).astype(BF16)
        return carry

    lax.fori_loop(0, places, scale, 0, unroll=2)
    inverse_copy.wait()

    def give(b, carry):
        arranged[b] = scaled[inverse[b]]
        return carry

    parts = 4
    size = blocks // parts
    for n in range(parts):
        lax.fori_loop(n * size, (n + 1) * size, give, 0, unroll=min(8, size))
        part = pl.ds(n * size, size)
        stores.append(pltpu.make_async_copy(arranged.at[part], update.at[part], sem.at[3 + n]))
        stores[-1].start()
    for store in stores:
        store.wait()


def body(nd, nm, grads, order, left_stat, right_stat, left_root, right_root):
    blocks, rows, cols = grads.shape
    _, half, width = left_stat.shape
    vmem = pl.BlockSpec(memory_space=pltpu.VMEM)
    half_shape = left_stat.shape
    hbm = pl.BlockSpec(memory_space=pltpu.HBM)
    dma = pltpu.SemaphoreType.DMA
    operands = [order.reshape(1, blocks), grads, left_stat, right_stat, left_root, right_root]
    operands = [pltpu.with_memory_space_constraint(x, pltpu.HBM) for x in operands]
    products = 4 * half * width * width
    results = pl.pallas_call(
        functools.partial(kernel, nd, nm),
        out_shape=(
            pltpu.VMEM(left_stat.shape, F32),
            pltpu.VMEM(right_stat.shape, F32),
            pltpu.VMEM(grads.shape, BF16),
            pltpu.VMEM((nd, 8, 128), F32),
            pltpu.VMEM((1, blocks), jnp.int32),
        ),
        in_specs=[hbm] * 6,
        out_specs=(vmem,) * 5,
        scratch_shapes=[
            pltpu.SMEM((blocks,), jnp.int32),
            pltpu.VMEM((1, blocks), jnp.int32),
            pltpu.VMEM((blocks, rows, cols), BF16),
            pltpu.VMEM((blocks, rows, cols), BF16),
            pltpu.VMEM((nm, width, cols), BF16),
            pltpu.VMEM((width, width), BF16),
            pltpu.VMEM((half, width), BF16),
            pltpu.VMEM((width, width), BF16),
            pltpu.VMEM((half, width), F32),
            pltpu.VMEM((half, cols), BF16),
            pltpu.VMEM((nm, half, cols), BF16),
            pltpu.VMEM((half, cols), BF16),
            pltpu.VMEM((nd, 8, 128), F32),
            pltpu.VMEM((8, 128), F32),
            pltpu.VMEM((nm, 8, 128), F32),
            pltpu.VMEM((8, 128), F32),
            pltpu.VMEM((nm, 8, 128), F32),
            dma((7,)),
            dma((nm, 4)),
            dma,
            dma,
            dma((2,)),
            dma((2,)),
            dma((2,)),
            dma((2,)),
            dma((2,)),
            dma,
            dma,
            dma((2,)),
            pltpu.SemaphoreType.REGULAR,
        ],
        compiler_params=pltpu.CompilerParams(
            collective_id=0, has_side_effects=True, vmem_limit_bytes=48 * 1024 * 1024
        ),
        cost_estimate=pl.CostEstimate(
            flops=2 * products, bytes_accessed=12 * half * width * 2, transcendentals=0
        ),
        name="step",
    )(*operands)
    return pl.pallas_call(
        finish_kernel,
        out_shape=(
            pltpu.HBM(half_shape, F32),
            pltpu.HBM(half_shape, F32),
            pltpu.HBM(grads.shape, BF16),
        ),
        in_specs=[vmem] * 5,
        out_specs=(hbm, hbm, hbm),
        scratch_shapes=[
            pltpu.SMEM((blocks,), jnp.int32),
            pltpu.VMEM(grads.shape, BF16),
            pltpu.VMEM(grads.shape, BF16),
            dma((7,)),
        ],
        compiler_params=pltpu.CompilerParams(vmem_limit_bytes=8 * 1024 * 1024),
        cost_estimate=pl.CostEstimate(flops=0, bytes_accessed=10 * half * width, transcendentals=0),
        name="finish",
    )(*results)


def solution(mesh):
    owned = P(("dp", "mp"), None, None)
    return jax.shard_map(
        functools.partial(body, mesh.shape["dp"], mesh.shape["mp"]),
        mesh=mesh,
        in_specs=(P(None, "dp", "mp"), P(), owned, owned, owned, owned),
        out_specs=(owned, owned, P(None, "dp", "mp")),
        check_vma=False,
    )
```

```python
import functools

import jax
import jax.numpy as jnp
from jax import lax
from jax.experimental import pallas as pl
from jax.experimental.pallas import tpu as pltpu
from jax.sharding import PartitionSpec as P

MESH = pl.DeviceIdType.MESH
F32 = jnp.float32
BF16 = jnp.bfloat16
beta_two = 0.95
clip_rms = 0.5


def fold(x):
    x = x.astype(F32)
    return jnp.sum((x * x).reshape(-1, 8, 128), axis=0)


def everything(x):
    return jnp.sum(jnp.sum(x, axis=0, keepdims=True), axis=1, keepdims=True)


def kernel(
    nd,
    nm,
    order_in,
    grads_in,
    left_stat,
    right_stat,
    left_root,
    right_root,
    new_left,
    new_right,
    u_in,
    scales,
    inverse,
    order,
    order_row,
    grads,
    tiles,
    slabs,
    full,
    lroot,
    rroot,
    acc,
    last_a,
    u_out,
    relay,
    sq_dp,
    sq_mine,
    sq_mp,
    g_sq,
    sums,
    load_sem,
    slab_sem,
    tile_sem,
    forward_sem,
    root_sem,
    sq_send_sem,
    sq_recv_sem,
    sum_send_sem,
    sum_recv_sem,
    u_send_sem,
    u_recv_sem,
    relay_sem,
    ready_sem,
):
    blocks, rows, cols = grads.shape
    half, width = lroot.shape
    pairs = nm // 2
    d = lax.axis_index("dp")
    m = lax.axis_index("mp")
    h = m % 2
    pair = m // 2
    sigma = 2 * h - 1
    partner = m - sigma
    per_half = nd // 2
    my_rows = pl.ds(pl.multiple_of(h * half, half), half)

    def place(offset):
        return (m + offset + 2 * nm) % nm

    first_loads = [
        pltpu.make_async_copy(order_in.at[0], order, load_sem.at[4]),
        pltpu.make_async_copy(grads_in, grads, load_sem.at[5]),
        pltpu.make_async_copy(order_in, order_row, load_sem.at[6]),
    ]
    for load in first_loads:
        load.start()

    barrier = pltpu.get_barrier_semaphore()

    def greet(k, carry):
        pl.semaphore_signal(barrier, inc=1, device_id=((d + k) % nd, m), device_id_type=MESH)
        return carry

    lax.fori_loop(1, nd, greet, 0)
    for k in range(1, nm):
        pl.semaphore_signal(barrier, inc=1, device_id=(d, (m + k) % nm), device_id_type=MESH)

    loads = [
        pltpu.make_async_copy(left_root.at[0], lroot, load_sem.at[0]),
        pltpu.make_async_copy(right_root.at[0], rroot.at[my_rows], load_sem.at[1]),
        pltpu.make_async_copy(left_stat, new_left, load_sem.at[2]),
        pltpu.make_async_copy(right_stat, new_right, load_sem.at[3]),
    ]

    pl.semaphore_wait(barrier, nd - 1 + nm - 1)
    for k in range(1, nm):
        pl.semaphore_signal(ready_sem, inc=1, device_id=(d, (m + k) % nm), device_id_type=MESH)

    part_rows = half // 4

    def root_copy(n):
        return pltpu.make_async_remote_copy(
            src_ref=right_root.at[0, pl.ds(n * part_rows, part_rows)],
            dst_ref=rroot.at[pl.ds(pl.multiple_of(h * half + n * part_rows, part_rows), part_rows)],
            send_sem=root_sem.at[0],
            recv_sem=root_sem.at[1],
            device_id=(d, partner),
            device_id_type=MESH,
        )

    root_copy(0).start()
    for load in loads:
        load.start()

    targets = [place(3 * sigma), place(-2 * sigma), place(sigma), m]

    groups = min(4, nd)
    group_places = nd // groups
    group_rows = width // groups
    group = d // group_places

    def tile_copy(there, target):
        return pltpu.make_async_remote_copy(
            src_ref=tiles.at[pairs * there + target // 2],
            dst_ref=slabs.at[m, pl.ds(pl.multiple_of(d * rows, rows), rows)],
            send_sem=tile_sem,
            recv_sem=slab_sem.at[m, group],
            device_id=(there, target),
            device_id_type=MESH,
        )

    def arrange(there, total):
        for p in range(pairs):
            s = pairs * there + p
            tile = grads[order[s]]
            tiles[s] = tile
            total = total + fold(tile)
        return total

    for load in first_loads:
        load.wait()
    pl.semaphore_wait(ready_sem, nm - 1)
    total = arrange(d, jnp.zeros((8, 128), F32))
    for target in targets[:3]:
        tile_copy(d, target).start()
    pltpu.make_async_copy(
        tiles.at[pairs * d + pair],
        slabs.at[m, pl.ds(pl.multiple_of(d * rows, rows), rows)],
        slab_sem.at[m, group],
    ).start()

    def send_tiles(k, total):
        there_group = (group - k // group_places + groups) % groups
        there = there_group * group_places + (d + 3 * k) % group_places
        total = arrange(there, total)
        for target in targets:
            tile_copy(there, target).start()
        return total

    sq_dp[d] = lax.fori_loop(1, nd, send_tiles, total)

    for n in range(1, 4):
        root_copy(n).start()

    def send_sq(k, carry):
        pltpu.make_async_remote_copy(
            src_ref=sq_dp.at[d],
            dst_ref=sq_dp.at[d],
            send_sem=sq_send_sem.at[0],
            recv_sem=sq_recv_sem.at[0],
            device_id=((d + k) % nd, m),
            device_id_type=MESH,
        ).start()
        return carry

    lax.fori_loop(1, nd, send_sq, 0)
    some = sq_dp.at[pl.ds(0, nd - 1)]
    pltpu.make_async_copy(some, some, sq_recv_sem.at[0]).wait()
    sq_mine[...] = jnp.sum(sq_dp[...], axis=0)
    sq_mp[m] = sq_mine[...]
    for k in range(1, nm):
        pltpu.make_async_remote_copy(
            src_ref=sq_mine,
            dst_ref=sq_mp.at[m],
            send_sem=sq_send_sem.at[1],
            recv_sem=sq_recv_sem.at[1],
            device_id=(d, (m + k) % nm),
            device_id_type=MESH,
        ).start()

    def part_of(k, g):
        return slabs.at[k, pl.ds(pl.multiple_of(g * group_rows, group_rows), group_rows)]

    def wait_part(k, g):
        pltpu.make_async_copy(part_of(k, g), part_of(k, g), slab_sem.at[k, g]).wait()

    def wait_slab(k):
        for g in range(groups):
            wait_part(k, g)

    def forward(c, carry):
        g = (group + c) % groups
        for j in range(pairs):
            k = place(j * sigma)
            wait_part(k, g)
            pltpu.make_async_remote_copy(
                src_ref=part_of(k, g),
                dst_ref=part_of(k, g),
                send_sem=forward_sem,
                recv_sem=slab_sem.at[k, g],
                device_id=(d, partner),
                device_id_type=MESH,
            ).start()
        return carry

    lax.fori_loop(0, groups, forward, 0)

    spread = jnp.transpose(jnp.broadcast_to(order_row[...], (blocks, blocks)))
    slot_of = lax.broadcasted_iota(jnp.int32, (blocks, blocks), 0)
    block_of = lax.broadcasted_iota(jnp.int32, (blocks, blocks), 1)
    inverse[...] = jnp.max(jnp.where(spread == block_of, slot_of, 0), axis=0, keepdims=True)

    loads[0].wait()
    loads[1].wait()
    pltpu.make_async_copy(lroot, lroot, root_sem.at[1]).wait()
    acc[...] = jnp.zeros_like(acc)
    g_sq[...] = jnp.zeros_like(g_sq)

    def through_left(k):
        slab = slabs[k]
        g_sq[...] += fold(slab)
        return jnp.dot(lroot[...], slab, preferred_element_type=F32).astype(BF16)

    def right_rows(k):
        return pl.ds(pl.multiple_of(k * cols, cols), cols)

    def use_slab(k):
        a = through_left(k)
        acc[...] += jnp.dot(a, rroot[right_rows(k)], preferred_element_type=F32)

    def near(j, carry):
        use_slab(place(j * sigma))
        return carry

    def far(j, carry):
        k = place(-(j + 1) * sigma)
        wait_slab(k)
        use_slab(k)
        return carry

    lax.fori_loop(0, pairs, near, 0)
    lax.fori_loop(0, pairs - 1, far, 0)
    last = place(-pairs * sigma)
    wait_slab(last)
    last_a[...] = through_left(last)
    step = 2 * cols

    opposite = place(nm // 2)

    def finish(i, total):
        n = (opposite // 2 + i) % pairs
        part = pl.ds(pl.multiple_of(n * step, step), step)
        u = acc[:, part] + jnp.dot(
            last_a[...], rroot[right_rows(last), part], preferred_element_type=F32
        )
        u_out[2 * n] = u[:, :cols].astype(BF16)
        u_out[2 * n + 1] = u[:, cols:].astype(BF16)
        return total + fold(u[:, :cols]) + fold(u[:, cols:])

    slot = pairs * d + pair

    def u_copy(near_row, target):
        return pltpu.make_async_remote_copy(
            src_ref=u_out.at[target, pl.ds(pl.multiple_of(near_row * rows, rows), rows)],
            dst_ref=u_in.at[slot],
            send_sem=u_send_sem,
            recv_sem=u_recv_sem,
            device_id=(h * per_half + near_row, target),
            device_id_type=MESH,
        )

    u_sq = finish(0, jnp.zeros((8, 128), F32))
    relay_copy = pltpu.make_async_remote_copy(
        src_ref=u_out.at[opposite],
        dst_ref=relay,
        send_sem=relay_sem.at[0],
        recv_sem=relay_sem.at[1],
        device_id=(d, partner),
        device_id_type=MESH,
    )
    relay_copy.start()
    beside = place(3 * sigma)

    def send_beside(k, carry):
        u_copy((d + 7 * k) % per_half, beside).start()
        return carry

    lax.fori_loop(0, per_half, send_beside, 0)
    u_sq = lax.fori_loop(1, pairs, finish, u_sq)

    row = lax.broadcasted_iota(jnp.int32, (8, 128), 0)
    sums[m] = jnp.where(row < 4, everything(u_sq), everything(g_sq[...]))
    for k in range(1, nm):
        pltpu.make_async_remote_copy(
            src_ref=sums.at[m],
            dst_ref=sums.at[m],
            send_sem=sum_send_sem.at[0],
            recv_sem=sum_recv_sem.at[0],
            device_id=(d, (m + k) % nm),
            device_id_type=MESH,
        ).start()

    own_half = d // per_half == h

    across = opposite // 2 + 1 - 2 * (opposite // 2 % 2)
    along = pair + 1 - 2 * (pair % 2)

    def send_across(k, carry):
        near_row = (d + 7 * k) % per_half
        for side in range(2):
            u_copy(near_row, 2 * across + side).start()
        return carry

    def send_u(k, carry):
        near_row = (d + 7 * k) % per_half
        for target in (2 * along, 2 * along + 1, partner):
            u_copy(near_row, target).start()
        here = jnp.logical_and(own_half, k == 0)

        @pl.when(here)
        def _():
            pltpu.make_async_copy(
                u_out.at[m, pl.ds(pl.multiple_of(near_row * rows, rows), rows)],
                u_in.at[slot],
                u_recv_sem,
            ).start()

        @pl.when(jnp.logical_not(here))
        def _():
            u_copy(near_row, m).start()

        return carry

    lax.fori_loop(0, per_half, send_across, 0)
    relay_copy.wait_recv()

    def pass_on(k, carry):
        near_row = (d + 7 * k) % per_half
        pltpu.make_async_remote_copy(
            src_ref=relay.at[pl.ds(pl.multiple_of(near_row * rows, rows), rows)],
            dst_ref=u_in.at[slot],
            send_sem=u_send_sem,
            recv_sem=u_recv_sem,
            device_id=((1 - h) * per_half + near_row, (partner + nm // 2) % nm),
            device_id_type=MESH,
        ).start()
        return carry

    lax.fori_loop(0, per_half, pass_on, 0)

    some_mp = sq_mp.at[pl.ds(0, nm - 1)]
    pltpu.make_async_copy(some_mp, some_mp, sq_recv_sem.at[1]).wait()
    total_sq = everything(jnp.sum(sq_mp[...], axis=0))
    clip = jnp.minimum(1.0, clip_rms * jnp.sqrt(F32(blocks * width * width)) / jnp.sqrt(total_sq + 1e-06))
    coefficient = (1.0 - beta_two) * clip * clip
    pltpu.make_async_copy(some_mp, some_mp, sum_recv_sem.at[0]).wait()
    mine = jnp.zeros((8, 128), F32)
    for p in range(pairs):
        u_total = sums[2 * p, 0:1] + sums[2 * p + 1, 0:1]
        scale = -(clip * jnp.sqrt(sums[2 * p, 4:5]) / jnp.sqrt(u_total + 1e-06))
        mine = jnp.where(row == p, scale, mine)
    scales[d] = mine

    def send_scales(k, carry):
        pltpu.make_async_remote_copy(
            src_ref=scales.at[d],
            dst_ref=scales.at[d],
            send_sem=sum_send_sem.at[1],
            recv_sem=sum_recv_sem.at[1],
            device_id=((d + k) % nd, m),
            device_id_type=MESH,
        ).start()
        return carry

    lax.fori_loop(1, nd, send_scales, 0)
    lax.fori_loop(0, per_half, send_u, 0)

    for k in range(nm):
        full[:, k * cols : (k + 1) * cols] = slabs[k]
    loads[2].wait()

    def left_gram(n, carry):
        part = pl.ds(pl.multiple_of(n * step, step), step)
        gram = lax.dot_general(
            full[my_rows], full[part], (((1,), (1,)), ((), ())), preferred_element_type=F32
        )
        new_left[0, :, part] = beta_two * new_left[0, :, part] + coefficient * gram
        return carry

    lax.fori_loop(0, width // step, left_gram, 0)
    loads[3].wait()

    def right_gram(n, carry):
        part = pl.ds(pl.multiple_of(n * step, step), step)
        gram = lax.dot_general(
            full[:, my_rows], full[:, part], (((0,), (0,)), ((), ())), preferred_element_type=F32
        )
        new_right[0, :, part] = beta_two * new_right[0, :, part] + coefficient * gram
        return carry

    lax.fori_loop(0, width // step, right_gram, 0)

    sent = tiles.at[pl.ds(0, blocks - 1)]
    pltpu.make_async_copy(sent, sent, tile_sem).wait()
    pltpu.make_async_copy(lroot, lroot, root_sem.at[0]).wait()
    pltpu.make_async_copy(some, some, sq_send_sem.at[0]).wait()
    pltpu.make_async_copy(some_mp, some_mp, sq_send_sem.at[1]).wait()
    pltpu.make_async_copy(some_mp, some_mp, sum_send_sem.at[0]).wait()
    pltpu.make_async_copy(some, some, sum_send_sem.at[1]).wait()
    relay_copy.wait_send()
    pltpu.make_async_copy(lroot, lroot, forward_sem).wait()

    @pl.when(own_half)
    def _():
        pltpu.make_async_copy(sent, sent, u_send_sem).wait()

    @pl.when(jnp.logical_not(own_half))
    def _():
        pltpu.make_async_copy(tiles, tiles, u_send_sem).wait()

    pltpu.make_async_copy(some, some, sum_recv_sem.at[1]).wait()
    pltpu.make_async_copy(u_in, u_in, u_recv_sem).wait()


def finish_kernel(
    left, right, tiles, scales, inverse_in, new_left, new_right, update, inverse, scaled, arranged, sem
):
    places = scales.shape[0]
    blocks = tiles.shape[0]
    pairs = blocks // places
    inverse_copy = pltpu.make_async_copy(inverse_in.at[0], inverse, sem.at[0])
    inverse_copy.start()
    parts = 4
    some = left.shape[1] // parts
    stores = []
    for n in range(parts):
        part = pl.ds(n * some, some)
        stores.append(pltpu.make_async_copy(left.at[:, part], new_left.at[:, part], sem.at[1 + n]))
        stores.append(pltpu.make_async_copy(right.at[:, part], new_right.at[:, part], sem.at[1 + parts + n]))
    for store in stores:
        store.start()

    def scale(there, carry):
        for p in range(pairs):
            s = pairs * there + p
            scaled[s] = (tiles[s].astype(F32) * scales[there, p : p + 1]).astype(BF16)
        return carry

    lax.fori_loop(0, places, scale, 0, unroll=2)
    inverse_copy.wait()

    def give(b, carry):
        arranged[b] = scaled[inverse[b]]
        return carry

    size = blocks // parts
    for n in range(parts):
        lax.fori_loop(n * size, (n + 1) * size, give, 0, unroll=min(8, size))
        part = pl.ds(n * size, size)
        stores.append(pltpu.make_async_copy(arranged.at[part], update.at[part], sem.at[1 + 2 * parts + n]))
        stores[-1].start()
    for store in stores:
        store.wait()


def body(nd, nm, grads, order, left_stat, right_stat, left_root, right_root):
    blocks, rows, cols = grads.shape
    _, half, width = left_stat.shape
    vmem = pl.BlockSpec(memory_space=pltpu.VMEM)
    half_shape = left_stat.shape
    hbm = pl.BlockSpec(memory_space=pltpu.HBM)
    dma = pltpu.SemaphoreType.DMA
    operands = [order.reshape(1, blocks), grads, left_stat, right_stat, left_root, right_root]
    operands = [pltpu.with_memory_space_constraint(x, pltpu.HBM) for x in operands]
    products = 4 * half * width * width
    results = pl.pallas_call(
        functools.partial(kernel, nd, nm),
        out_shape=(
            pltpu.VMEM(left_stat.shape, F32),
            pltpu.VMEM(right_stat.shape, F32),
            pltpu.VMEM(grads.shape, BF16),
            pltpu.VMEM((nd, 8, 128), F32),
            pltpu.VMEM((1, blocks), jnp.int32),
        ),
        in_specs=[hbm] * 6,
        out_specs=(vmem,) * 5,
        scratch_shapes=[
            pltpu.SMEM((blocks,), jnp.int32),
            pltpu.VMEM((1, blocks), jnp.int32),
            pltpu.VMEM((blocks, rows, cols), BF16),
            pltpu.VMEM((blocks, rows, cols), BF16),
            pltpu.VMEM((nm, width, cols), BF16),
            pltpu.VMEM((width, width), BF16),
            pltpu.VMEM((half, width), BF16),
            pltpu.VMEM((width, width), BF16),
            pltpu.VMEM((half, width), F32),
            pltpu.VMEM((half, cols), BF16),
            pltpu.VMEM((nm, half, cols), BF16),
            pltpu.VMEM((half, cols), BF16),
            pltpu.VMEM((nd, 8, 128), F32),
            pltpu.VMEM((8, 128), F32),
            pltpu.VMEM((nm, 8, 128), F32),
            pltpu.VMEM((8, 128), F32),
            pltpu.VMEM((nm, 8, 128), F32),
            dma((7,)),
            dma((nm, 4)),
            dma,
            dma,
            dma((2,)),
            dma((2,)),
            dma((2,)),
            dma((2,)),
            dma((2,)),
            dma,
            dma,
            dma((2,)),
            pltpu.SemaphoreType.REGULAR,
        ],
        compiler_params=pltpu.CompilerParams(
            collective_id=0, has_side_effects=True, vmem_limit_bytes=48 * 1024 * 1024
        ),
        cost_estimate=pl.CostEstimate(
            flops=2 * products, bytes_accessed=12 * half * width * 2, transcendentals=0
        ),
        name="step",
    )(*operands)
    return pl.pallas_call(
        finish_kernel,
        out_shape=(
            pltpu.HBM(half_shape, F32),
            pltpu.HBM(half_shape, F32),
            pltpu.HBM(grads.shape, BF16),
        ),
        in_specs=[vmem] * 5,
        out_specs=(hbm, hbm, hbm),
        scratch_shapes=[
            pltpu.SMEM((blocks,), jnp.int32),
            pltpu.VMEM(grads.shape, BF16),
            pltpu.VMEM(grads.shape, BF16),
            dma((13,)),
        ],
        compiler_params=pltpu.CompilerParams(vmem_limit_bytes=8 * 1024 * 1024),
        cost_estimate=pl.CostEstimate(flops=0, bytes_accessed=10 * half * width, transcendentals=0),
        name="finish",
    )(*results)


def solution(mesh):
    owned = P(("dp", "mp"), None, None)
    return jax.shard_map(
        functools.partial(body, mesh.shape["dp"], mesh.shape["mp"]),
        mesh=mesh,
        in_specs=(P(None, "dp", "mp"), P(), owned, owned, owned, owned),
        out_specs=(owned, owned, P(None, "dp", "mp")),
        check_vma=False,
    )
```

```python
import functools

import jax
import jax.numpy as jnp
from jax import lax
from jax.experimental import pallas as pl
from jax.experimental.pallas import tpu as pltpu
from jax.sharding import PartitionSpec as P

MESH = pl.DeviceIdType.MESH
F32 = jnp.float32
BF16 = jnp.bfloat16
beta_two = 0.95
clip_rms = 0.5


def fold(x):
    x = x.astype(F32)
    return jnp.sum((x * x).reshape(-1, 8, 128), axis=0)


def everything(x):
    return jnp.sum(jnp.sum(x, axis=0, keepdims=True), axis=1, keepdims=True)


def kernel(
    nd,
    nm,
    order_in,
    grads_in,
    left_stat,
    right_stat,
    left_root,
    right_root,
    new_left,
    new_right,
    u_in,
    scales,
    inverse,
    order,
    order_row,
    grads,
    tiles,
    slabs,
    full,
    lroot,
    rroot,
    acc,
    last_a,
    u_out,
    relay,
    sq_dp,
    sq_mine,
    sq_mp,
    g_sq,
    sums,
    load_sem,
    slab_sem,
    tile_sem,
    forward_sem,
    root_sem,
    sq_send_sem,
    sq_recv_sem,
    sum_send_sem,
    sum_recv_sem,
    u_send_sem,
    u_recv_sem,
    relay_sem,
    ready_sem,
):
    blocks, rows, cols = grads.shape
    half, width = lroot.shape
    pairs = nm // 2
    d = lax.axis_index("dp")
    m = lax.axis_index("mp")
    h = m % 2
    pair = m // 2
    sigma = 2 * h - 1
    partner = m - sigma
    per_half = nd // 2
    my_rows = pl.ds(pl.multiple_of(h * half, half), half)

    def place(offset):
        return (m + offset + 2 * nm) % nm

    first_loads = [
        pltpu.make_async_copy(order_in.at[0], order, load_sem.at[4]),
        pltpu.make_async_copy(grads_in, grads, load_sem.at[5]),
        pltpu.make_async_copy(order_in, order_row, load_sem.at[6]),
    ]
    for load in first_loads:
        load.start()

    barrier = pltpu.get_barrier_semaphore()

    def greet(k, carry):
        pl.semaphore_signal(barrier, inc=1, device_id=((d + k) % nd, m), device_id_type=MESH)
        return carry

    lax.fori_loop(1, nd, greet, 0)
    for k in range(1, nm):
        pl.semaphore_signal(barrier, inc=1, device_id=(d, (m + k) % nm), device_id_type=MESH)

    loads = [
        pltpu.make_async_copy(left_root.at[0], lroot, load_sem.at[0]),
        pltpu.make_async_copy(right_root.at[0], rroot.at[my_rows], load_sem.at[1]),
        pltpu.make_async_copy(left_stat, new_left, load_sem.at[2]),
        pltpu.make_async_copy(right_stat, new_right, load_sem.at[3]),
    ]

    pl.semaphore_wait(barrier, nd - 1 + nm - 1)
    for k in range(1, nm):
        pl.semaphore_signal(ready_sem, inc=1, device_id=(d, (m + k) % nm), device_id_type=MESH)

    part_rows = half // 4

    def root_copy(n):
        return pltpu.make_async_remote_copy(
            src_ref=right_root.at[0, pl.ds(n * part_rows, part_rows)],
            dst_ref=rroot.at[pl.ds(pl.multiple_of(h * half + n * part_rows, part_rows), part_rows)],
            send_sem=root_sem.at[0],
            recv_sem=root_sem.at[1],
            device_id=(d, partner),
            device_id_type=MESH,
        )

    root_copy(0).start()
    for load in loads:
        load.start()

    targets = [place(3 * sigma), place(-2 * sigma), place(sigma), m]

    groups = min(4, nd)
    group_places = nd // groups
    group_rows = width // groups
    group = d // group_places

    def tile_copy(there, target):
        return pltpu.make_async_remote_copy(
            src_ref=tiles.at[pairs * there + target // 2],
            dst_ref=slabs.at[m, pl.ds(pl.multiple_of(d * rows, rows), rows)],
            send_sem=tile_sem,
            recv_sem=slab_sem.at[m, group],
            device_id=(there, target),
            device_id_type=MESH,
        )

    def arrange(there, total):
        for p in range(pairs):
            s = pairs * there + p
            tile = grads[order[s]]
            tiles[s] = tile
            total = total + fold(tile)
        return total

    for load in first_loads:
        load.wait()
    pl.semaphore_wait(ready_sem, nm - 1)
    total = arrange(d, jnp.zeros((8, 128), F32))
    for target in targets[:3]:
        tile_copy(d, target).start()
    pltpu.make_async_copy(
        tiles.at[pairs * d + pair],
        slabs.at[m, pl.ds(pl.multiple_of(d * rows, rows), rows)],
        slab_sem.at[m, group],
    ).start()

    def send_tiles(k, total):
        there_group = (group - k // group_places + groups) % groups
        there = there_group * group_places + (d + 3 * k) % group_places
        total = arrange(there, total)
        for target in targets:
            tile_copy(there, target).start()
        return total

    sq_dp[d] = lax.fori_loop(1, nd, send_tiles, total)

    for n in range(1, 4):
        root_copy(n).start()

    def send_sq(k, carry):
        pltpu.make_async_remote_copy(
            src_ref=sq_dp.at[d],
            dst_ref=sq_dp.at[d],
            send_sem=sq_send_sem.at[0],
            recv_sem=sq_recv_sem.at[0],
            device_id=((d + k) % nd, m),
            device_id_type=MESH,
        ).start()
        return carry

    lax.fori_loop(1, nd, send_sq, 0)
    some = sq_dp.at[pl.ds(0, nd - 1)]
    pltpu.make_async_copy(some, some, sq_recv_sem.at[0]).wait()
    sq_mine[...] = jnp.sum(sq_dp[...], axis=0)
    sq_mp[m] = sq_mine[...]
    for k in range(1, nm):
        pltpu.make_async_remote_copy(
            src_ref=sq_mine,
            dst_ref=sq_mp.at[m],
            send_sem=sq_send_sem.at[1],
            recv_sem=sq_recv_sem.at[1],
            device_id=(d, (m + k) % nm),
            device_id_type=MESH,
        ).start()

    def part_of(k, g):
        return slabs.at[k, pl.ds(pl.multiple_of(g * group_rows, group_rows), group_rows)]

    def wait_part(k, g):
        pltpu.make_async_copy(part_of(k, g), part_of(k, g), slab_sem.at[k, g]).wait()

    def wait_slab(k):
        for g in range(groups):
            wait_part(k, g)

    def forward(c, carry):
        g = (group + c) % groups
        for j in range(pairs):
            k = place(j * sigma)
            wait_part(k, g)
            pltpu.make_async_remote_copy(
                src_ref=part_of(k, g),
                dst_ref=part_of(k, g),
                send_sem=forward_sem,
                recv_sem=slab_sem.at[k, g],
                device_id=(d, partner),
                device_id_type=MESH,
            ).start()
        return carry

    lax.fori_loop(0, groups, forward, 0)

    spread = jnp.transpose(jnp.broadcast_to(order_row[...], (blocks, blocks)))
    slot_of = lax.broadcasted_iota(jnp.int32, (blocks, blocks), 0)
    block_of = lax.broadcasted_iota(jnp.int32, (blocks, blocks), 1)
    inverse[...] = jnp.max(jnp.where(spread == block_of, slot_of, 0), axis=0, keepdims=True)

    loads[0].wait()
    loads[1].wait()
    pltpu.make_async_copy(lroot, lroot, root_sem.at[1]).wait()
    acc[...] = jnp.zeros_like(acc)
    g_sq[...] = jnp.zeros_like(g_sq)

    def through_left(k):
        slab = slabs[k]
        g_sq[...] += fold(slab)
        return jnp.dot(lroot[...], slab, preferred_element_type=F32).astype(BF16)

    def right_rows(k):
        return pl.ds(pl.multiple_of(k * cols, cols), cols)

    def use_slab(k):
        a = through_left(k)
        acc[...] += jnp.dot(a, rroot[right_rows(k)], preferred_element_type=F32)

    def near(j, carry):
        use_slab(place(j * sigma))
        return carry

    def far(j, carry):
        k = place(-(j + 1) * sigma)
        wait_slab(k)
        use_slab(k)
        return carry

    lax.fori_loop(0, pairs, near, 0)
    lax.fori_loop(0, pairs - 1, far, 0)
    last = place(-pairs * sigma)
    wait_slab(last)
    last_a[...] = through_left(last)
    step = 2 * cols

    opposite = place(nm // 2)

    def finish(i, total):
        n = (opposite // 2 + i) % pairs
        part = pl.ds(pl.multiple_of(n * step, step), step)
        u = acc[:, part] + jnp.dot(
            last_a[...], rroot[right_rows(last), part], preferred_element_type=F32
        )
        u_out[2 * n] = u[:, :cols].astype(BF16)
        u_out[2 * n + 1] = u[:, cols:].astype(BF16)
        return total + fold(u[:, :cols]) + fold(u[:, cols:])

    slot = pairs * d + pair

    def u_copy(near_row, target):
        return pltpu.make_async_remote_copy(
            src_ref=u_out.at[target, pl.ds(pl.multiple_of(near_row * rows, rows), rows)],
            dst_ref=u_in.at[slot],
            send_sem=u_send_sem,
            recv_sem=u_recv_sem,
            device_id=(h * per_half + near_row, target),
            device_id_type=MESH,
        )

    u_sq = finish(0, jnp.zeros((8, 128), F32))
    relay_copy = pltpu.make_async_remote_copy(
        src_ref=u_out.at[opposite],
        dst_ref=relay,
        send_sem=relay_sem.at[0],
        recv_sem=relay_sem.at[1],
        device_id=(d, partner),
        device_id_type=MESH,
    )
    relay_copy.start()
    u_sq = lax.fori_loop(1, pairs, finish, u_sq)

    row = lax.broadcasted_iota(jnp.int32, (8, 128), 0)
    sums[m] = jnp.where(row < 4, everything(u_sq), everything(g_sq[...]))
    for k in range(1, nm):
        pltpu.make_async_remote_copy(
            src_ref=sums.at[m],
            dst_ref=sums.at[m],
            send_sem=sum_send_sem.at[0],
            recv_sem=sum_recv_sem.at[0],
            device_id=(d, (m + k) % nm),
            device_id_type=MESH,
        ).start()

    own_half = d // per_half == h

    def send_u(k, carry):
        near_row = (d + 7 * k) % per_half
        for i, j in enumerate((3, -3, 2, -2, 1, -1)):
            u_copy((near_row + 5 * i + 3) % per_half, place(j * sigma)).start()
        here = jnp.logical_and(own_half, k == 0)

        @pl.when(here)
        def _():
            pltpu.make_async_copy(
                u_out.at[m, pl.ds(pl.multiple_of(near_row * rows, rows), rows)],
                u_in.at[slot],
                u_recv_sem,
            ).start()

        @pl.when(jnp.logical_not(here))
        def _():
            u_copy(near_row, m).start()

        return carry

    lax.fori_loop(0, per_half // 2, send_u, 0)
    relay_copy.wait_recv()

    def pass_on(k, carry):
        near_row = (d + 7 * k + 1) % per_half
        pltpu.make_async_remote_copy(
            src_ref=relay.at[pl.ds(pl.multiple_of(near_row * rows, rows), rows)],
            dst_ref=u_in.at[slot],
            send_sem=u_send_sem,
            recv_sem=u_recv_sem,
            device_id=((1 - h) * per_half + near_row, (partner + nm // 2) % nm),
            device_id_type=MESH,
        ).start()
        return carry


    some_mp = sq_mp.at[pl.ds(0, nm - 1)]
    pltpu.make_async_copy(some_mp, some_mp, sq_recv_sem.at[1]).wait()
    total_sq = everything(jnp.sum(sq_mp[...], axis=0))
    clip = jnp.minimum(1.0, clip_rms * jnp.sqrt(F32(blocks * width * width)) / jnp.sqrt(total_sq + 1e-06))
    coefficient = (1.0 - beta_two) * clip * clip
    pltpu.make_async_copy(some_mp, some_mp, sum_recv_sem.at[0]).wait()
    mine = jnp.zeros((8, 128), F32)
    for p in range(pairs):
        u_total = sums[2 * p, 0:1] + sums[2 * p + 1, 0:1]
        scale = -(clip * jnp.sqrt(sums[2 * p, 4:5]) / jnp.sqrt(u_total + 1e-06))
        mine = jnp.where(row == p, scale, mine)
    scales[d] = mine

    def send_scales(k, carry):
        pltpu.make_async_remote_copy(
            src_ref=scales.at[d],
            dst_ref=scales.at[d],
            send_sem=sum_send_sem.at[1],
            recv_sem=sum_recv_sem.at[1],
            device_id=((d + k) % nd, m),
            device_id_type=MESH,
        ).start()
        return carry

    lax.fori_loop(1, nd, send_scales, 0)

    def send_both(k, carry):
        pass_on(2 * k - per_half, 0)
        send_u(k, carry)
        return pass_on(2 * k - per_half + 1, carry)

    if per_half % 2:
        pass_on(0, 0)
        lax.fori_loop(0, per_half, send_u, 0)
    else:
        lax.fori_loop(per_half // 2, per_half, send_both, 0)

    for k in range(nm):
        full[:, k * cols : (k + 1) * cols] = slabs[k]
    loads[2].wait()

    def left_gram(n, carry):
        part = pl.ds(pl.multiple_of(n * step, step), step)
        gram = lax.dot_general(
            full[my_rows], full[part], (((1,), (1,)), ((), ())), preferred_element_type=F32
        )
        new_left[0, :, part] = beta_two * new_left[0, :, part] + coefficient * gram
        return carry

    lax.fori_loop(0, width // step, left_gram, 0)
    loads[3].wait()

    def right_gram(n, carry):
        part = pl.ds(pl.multiple_of(n * step, step), step)
        gram = lax.dot_general(
            full[:, my_rows], full[:, part], (((0,), (0,)), ((), ())), preferred_element_type=F32
        )
        new_right[0, :, part] = beta_two * new_right[0, :, part] + coefficient * gram
        return carry

    lax.fori_loop(0, width // step, right_gram, 0)

    sent = tiles.at[pl.ds(0, blocks - 1)]
    pltpu.make_async_copy(sent, sent, tile_sem).wait()
    pltpu.make_async_copy(lroot, lroot, root_sem.at[0]).wait()
    pltpu.make_async_copy(some, some, sq_send_sem.at[0]).wait()
    pltpu.make_async_copy(some_mp, some_mp, sq_send_sem.at[1]).wait()
    pltpu.make_async_copy(some_mp, some_mp, sum_send_sem.at[0]).wait()
    pltpu.make_async_copy(some, some, sum_send_sem.at[1]).wait()
    relay_copy.wait_send()
    pltpu.make_async_copy(lroot, lroot, forward_sem).wait()

    @pl.when(own_half)
    def _():
        pltpu.make_async_copy(sent, sent, u_send_sem).wait()

    @pl.when(jnp.logical_not(own_half))
    def _():
        pltpu.make_async_copy(tiles, tiles, u_send_sem).wait()

    pltpu.make_async_copy(some, some, sum_recv_sem.at[1]).wait()
    pltpu.make_async_copy(u_in, u_in, u_recv_sem).wait()


def finish_kernel(
    left, right, tiles, scales, inverse_in, new_left, new_right, update, inverse, scaled, arranged, sem
):
    places = scales.shape[0]
    blocks = tiles.shape[0]
    pairs = blocks // places
    inverse_copy = pltpu.make_async_copy(inverse_in.at[0], inverse, sem.at[0])
    inverse_copy.start()
    stores = [
        pltpu.make_async_copy(left, new_left, sem.at[1]),
        pltpu.make_async_copy(right, new_right, sem.at[2]),
    ]
    for store in stores:
        store.start()

    def scale(there, carry):
        for p in range(pairs):
            s = pairs * there + p
            scaled[s] = (tiles[s].astype(F32) * scales[there, p : p + 1]).astype(BF16)
        return carry

    lax.fori_loop(0, places, scale, 0, unroll=2)
    inverse_copy.wait()

    def give(b, carry):
        arranged[b] = scaled[inverse[b]]
        return carry

    parts = 4
    size = blocks // parts
    for n in range(parts):
        lax.fori_loop(n * size, (n + 1) * size, give, 0, unroll=min(8, size))
        part = pl.ds(n * size, size)
        stores.append(pltpu.make_async_copy(arranged.at[part], update.at[part], sem.at[3 + n]))
        stores[-1].start()
    for store in stores:
        store.wait()


def body(nd, nm, grads, order, left_stat, right_stat, left_root, right_root):
    blocks, rows, cols = grads.shape
    _, half, width = left_stat.shape
    vmem = pl.BlockSpec(memory_space=pltpu.VMEM)
    half_shape = left_stat.shape
    hbm = pl.BlockSpec(memory_space=pltpu.HBM)
    dma = pltpu.SemaphoreType.DMA
    operands = [order.reshape(1, blocks), grads, left_stat, right_stat, left_root, right_root]
    operands = [pltpu.with_memory_space_constraint(x, pltpu.HBM) for x in operands]
    products = 4 * half * width * width
    results = pl.pallas_call(
        functools.partial(kernel, nd, nm),
        out_shape=(
            pltpu.VMEM(left_stat.shape, F32),
            pltpu.VMEM(right_stat.shape, F32),
            pltpu.VMEM(grads.shape, BF16),
            pltpu.VMEM((nd, 8, 128), F32),
            pltpu.VMEM((1, blocks), jnp.int32),
        ),
        in_specs=[hbm] * 6,
        out_specs=(vmem,) * 5,
        scratch_shapes=[
            pltpu.SMEM((blocks,), jnp.int32),
            pltpu.VMEM((1, blocks), jnp.int32),
            pltpu.VMEM((blocks, rows, cols), BF16),
            pltpu.VMEM((blocks, rows, cols), BF16),
            pltpu.VMEM((nm, width, cols), BF16),
            pltpu.VMEM((width, width), BF16),
            pltpu.VMEM((half, width), BF16),
            pltpu.VMEM((width, width), BF16),
            pltpu.VMEM((half, width), F32),
            pltpu.VMEM((half, cols), BF16),
            pltpu.VMEM((nm, half, cols), BF16),
            pltpu.VMEM((half, cols), BF16),
            pltpu.VMEM((nd, 8, 128), F32),
            pltpu.VMEM((8, 128), F32),
            pltpu.VMEM((nm, 8, 128), F32),
            pltpu.VMEM((8, 128), F32),
            pltpu.VMEM((nm, 8, 128), F32),
            dma((7,)),
            dma((nm, 4)),
            dma,
            dma,
            dma((2,)),
            dma((2,)),
            dma((2,)),
            dma((2,)),
            dma((2,)),
            dma,
            dma,
            dma((2,)),
            pltpu.SemaphoreType.REGULAR,
        ],
        compiler_params=pltpu.CompilerParams(
            collective_id=0, has_side_effects=True, vmem_limit_bytes=48 * 1024 * 1024
        ),
        cost_estimate=pl.CostEstimate(
            flops=2 * products, bytes_accessed=12 * half * width * 2, transcendentals=0
        ),
        name="step",
    )(*operands)
    return pl.pallas_call(
        finish_kernel,
        out_shape=(
            pltpu.HBM(half_shape, F32),
            pltpu.HBM(half_shape, F32),
            pltpu.HBM(grads.shape, BF16),
        ),
        in_specs=[vmem] * 5,
        out_specs=(hbm, hbm, hbm),
        scratch_shapes=[
            pltpu.SMEM((blocks,), jnp.int32),
            pltpu.VMEM(grads.shape, BF16),
            pltpu.VMEM(grads.shape, BF16),
            dma((7,)),
        ],
        compiler_params=pltpu.CompilerParams(vmem_limit_bytes=8 * 1024 * 1024),
        cost_estimate=pl.CostEstimate(flops=0, bytes_accessed=10 * half * width, transcendentals=0),
        name="finish",
    )(*results)


def solution(mesh):
    owned = P(("dp", "mp"), None, None)
    return jax.shard_map(
        functools.partial(body, mesh.shape["dp"], mesh.shape["mp"]),
        mesh=mesh,
        in_specs=(P(None, "dp", "mp"), P(), owned, owned, owned, owned),
        out_specs=(owned, owned, P(None, "dp", "mp")),
        check_vma=False,
    )
```

```python
import functools

import jax
import jax.numpy as jnp
from jax import lax
from jax.experimental import pallas as pl
from jax.experimental.pallas import tpu as pltpu
from jax.sharding import PartitionSpec as P

MESH = pl.DeviceIdType.MESH
F32 = jnp.float32
BF16 = jnp.bfloat16
beta_two = 0.95
clip_rms = 0.5


def fold(x):
    x = x.astype(F32)
    return jnp.sum((x * x).reshape(-1, 8, 128), axis=0)


def everything(x):
    return jnp.sum(jnp.sum(x, axis=0, keepdims=True), axis=1, keepdims=True)


def kernel(
    nd,
    nm,
    order_in,
    grads_in,
    left_stat,
    right_stat,
    left_root,
    right_root,
    new_left,
    new_right,
    u_in,
    scales,
    inverse,
    order,
    order_row,
    grads,
    tiles,
    slabs,
    full,
    lroot,
    rroot,
    acc,
    last_a,
    u_out,
    relay,
    sq_dp,
    sq_mine,
    sq_mp,
    g_sq,
    sums,
    load_sem,
    slab_sem,
    tile_sem,
    forward_sem,
    root_sem,
    sq_send_sem,
    sq_recv_sem,
    sum_send_sem,
    sum_recv_sem,
    u_send_sem,
    u_recv_sem,
    relay_sem,
    ready_sem,
):
    blocks, rows, cols = grads.shape
    half, width = lroot.shape
    pairs = nm // 2
    d = lax.axis_index("dp")
    m = lax.axis_index("mp")
    h = m % 2
    pair = m // 2
    sigma = 2 * h - 1
    partner = m - sigma
    per_half = nd // 2
    my_rows = pl.ds(pl.multiple_of(h * half, half), half)

    def place(offset):
        return (m + offset + 2 * nm) % nm

    first_loads = [
        pltpu.make_async_copy(order_in.at[0], order, load_sem.at[4]),
        pltpu.make_async_copy(grads_in, grads, load_sem.at[5]),
        pltpu.make_async_copy(order_in, order_row, load_sem.at[6]),
    ]
    for load in first_loads:
        load.start()

    barrier = pltpu.get_barrier_semaphore()

    def greet(k, carry):
        pl.semaphore_signal(barrier, inc=1, device_id=((d + k) % nd, m), device_id_type=MESH)
        return carry

    lax.fori_loop(1, nd, greet, 0)
    for k in range(1, nm):
        pl.semaphore_signal(barrier, inc=1, device_id=(d, (m + k) % nm), device_id_type=MESH)

    loads = [
        pltpu.make_async_copy(left_root.at[0], lroot, load_sem.at[0]),
        pltpu.make_async_copy(right_root.at[0], rroot.at[my_rows], load_sem.at[1]),
        pltpu.make_async_copy(left_stat, new_left, load_sem.at[2]),
        pltpu.make_async_copy(right_stat, new_right, load_sem.at[3]),
    ]

    pl.semaphore_wait(barrier, nd - 1 + nm - 1)
    for k in range(1, nm):
        pl.semaphore_signal(ready_sem, inc=1, device_id=(d, (m + k) % nm), device_id_type=MESH)

    part_rows = half // 4

    def root_copy(n):
        return pltpu.make_async_remote_copy(
            src_ref=right_root.at[0, pl.ds(n * part_rows, part_rows)],
            dst_ref=rroot.at[pl.ds(pl.multiple_of(h * half + n * part_rows, part_rows), part_rows)],
            send_sem=root_sem.at[0],
            recv_sem=root_sem.at[1],
            device_id=(d, partner),
            device_id_type=MESH,
        )

    root_copy(0).start()
    for load in loads:
        load.start()

    targets = [place(3 * sigma), place(-2 * sigma), place(sigma), m]

    groups = min(4, nd)
    group_places = nd // groups
    group_rows = width // groups
    group = d // group_places

    def tile_copy(there, target):
        return pltpu.make_async_remote_copy(
            src_ref=tiles.at[pairs * there + target // 2],
            dst_ref=slabs.at[m, pl.ds(pl.multiple_of(d * rows, rows), rows)],
            send_sem=tile_sem,
            recv_sem=slab_sem.at[m, group],
            device_id=(there, target),
            device_id_type=MESH,
        )

    def arrange(there, total):
        for p in range(pairs):
            s = pairs * there + p
            tile = grads[order[s]]
            tiles[s] = tile
            total = total + fold(tile)
        return total

    for load in first_loads:
        load.wait()
    pl.semaphore_wait(ready_sem, nm - 1)
    total = arrange(d, jnp.zeros((8, 128), F32))
    for target in targets[:3]:
        tile_copy(d, target).start()
    pltpu.make_async_copy(
        tiles.at[pairs * d + pair],
        slabs.at[m, pl.ds(pl.multiple_of(d * rows, rows), rows)],
        slab_sem.at[m, group],
    ).start()

    def send_tiles(k, total):
        there_group = (group - k // group_places + groups) % groups
        there = there_group * group_places + (d + 3 * k) % group_places
        total = arrange(there, total)
        for target in targets:
            tile_copy(there, target).start()
        return total

    sq_dp[d] = lax.fori_loop(1, nd, send_tiles, total)

    for n in range(1, 4):
        root_copy(n).start()

    def send_sq(k, carry):
        pltpu.make_async_remote_copy(
            src_ref=sq_dp.at[d],
            dst_ref=sq_dp.at[d],
            send_sem=sq_send_sem.at[0],
            recv_sem=sq_recv_sem.at[0],
            device_id=((d + k) % nd, m),
            device_id_type=MESH,
        ).start()
        return carry

    lax.fori_loop(1, nd, send_sq, 0)
    some = sq_dp.at[pl.ds(0, nd - 1)]
    pltpu.make_async_copy(some, some, sq_recv_sem.at[0]).wait()
    sq_mine[...] = jnp.sum(sq_dp[...], axis=0)
    sq_mp[m] = sq_mine[...]
    for k in range(1, nm):
        pltpu.make_async_remote_copy(
            src_ref=sq_mine,
            dst_ref=sq_mp.at[m],
            send_sem=sq_send_sem.at[1],
            recv_sem=sq_recv_sem.at[1],
            device_id=(d, (m + k) % nm),
            device_id_type=MESH,
        ).start()

    def part_of(k, g):
        return slabs.at[k, pl.ds(pl.multiple_of(g * group_rows, group_rows), group_rows)]

    def wait_part(k, g):
        pltpu.make_async_copy(part_of(k, g), part_of(k, g), slab_sem.at[k, g]).wait()

    def wait_slab(k):
        for g in range(groups):
            wait_part(k, g)

    def forward(c, carry):
        g = (group + c) % groups
        for j in range(pairs):
            k = place(j * sigma)
            wait_part(k, g)
            pltpu.make_async_remote_copy(
                src_ref=part_of(k, g),
                dst_ref=part_of(k, g),
                send_sem=forward_sem,
                recv_sem=slab_sem.at[k, g],
                device_id=(d, partner),
                device_id_type=MESH,
            ).start()
        return carry

    lax.fori_loop(0, groups, forward, 0)

    spread = jnp.transpose(jnp.broadcast_to(order_row[...], (blocks, blocks)))
    slot_of = lax.broadcasted_iota(jnp.int32, (blocks, blocks), 0)
    block_of = lax.broadcasted_iota(jnp.int32, (blocks, blocks), 1)
    inverse[...] = jnp.max(jnp.where(spread == block_of, slot_of, 0), axis=0, keepdims=True)

    loads[0].wait()
    loads[1].wait()
    pltpu.make_async_copy(lroot, lroot, root_sem.at[1]).wait()
    acc[...] = jnp.zeros_like(acc)
    g_sq[...] = jnp.zeros_like(g_sq)

    def through_left(k):
        slab = slabs[k]
        g_sq[...] += fold(slab)
        return jnp.dot(lroot[...], slab, preferred_element_type=F32).astype(BF16)

    def right_rows(k):
        return pl.ds(pl.multiple_of(k * cols, cols), cols)

    def use_slab(k):
        a = through_left(k)
        acc[...] += jnp.dot(a, rroot[right_rows(k)], preferred_element_type=F32)

    def near(j, carry):
        use_slab(place(j * sigma))
        return carry

    def far(j, carry):
        k = place(-(j + 1) * sigma)
        wait_slab(k)
        use_slab(k)
        return carry

    lax.fori_loop(0, pairs, near, 0)
    lax.fori_loop(0, pairs - 1, far, 0)
    last = place(-pairs * sigma)
    wait_slab(last)
    last_a[...] = through_left(last)
    step = 2 * cols

    opposite = place(nm // 2)

    def finish(i, total):
        n = (opposite // 2 + i) % pairs
        part = pl.ds(pl.multiple_of(n * step, step), step)
        u = acc[:, part] + jnp.dot(
            last_a[...], rroot[right_rows(last), part], preferred_element_type=F32
        )
        u_out[2 * n] = u[:, :cols].astype(BF16)
        u_out[2 * n + 1] = u[:, cols:].astype(BF16)
        return total + fold(u[:, :cols]) + fold(u[:, cols:])

    slot = pairs * d + pair

    def u_copy(near_row, target):
        return pltpu.make_async_remote_copy(
            src_ref=u_out.at[target, pl.ds(pl.multiple_of(near_row * rows, rows), rows)],
            dst_ref=u_in.at[slot],
            send_sem=u_send_sem,
            recv_sem=u_recv_sem,
            device_id=(h * per_half + near_row, target),
            device_id_type=MESH,
        )

    u_sq = finish(0, jnp.zeros((8, 128), F32))
    relay_copy = pltpu.make_async_remote_copy(
        src_ref=u_out.at[opposite],
        dst_ref=relay,
        send_sem=relay_sem.at[0],
        recv_sem=relay_sem.at[1],
        device_id=(d, partner),
        device_id_type=MESH,
    )
    relay_copy.start()
    beside = place(3 * sigma)

    def send_beside(k, carry):
        u_copy((d + 7 * k) % per_half, beside).start()
        return carry

    lax.fori_loop(0, per_half, send_beside, 0)
    u_sq = lax.fori_loop(1, pairs, finish, u_sq)

    row = lax.broadcasted_iota(jnp.int32, (8, 128), 0)
    sums[m] = jnp.where(row < 4, everything(u_sq), everything(g_sq[...]))
    for k in range(1, nm):
        pltpu.make_async_remote_copy(
            src_ref=sums.at[m],
            dst_ref=sums.at[m],
            send_sem=sum_send_sem.at[0],
            recv_sem=sum_recv_sem.at[0],
            device_id=(d, (m + k) % nm),
            device_id_type=MESH,
        ).start()

    own_half = d // per_half == h

    def send_u(k, carry):
        near_row = (d + 7 * k) % per_half
        for j in (-3, 2, -2, 1, -1):
            u_copy(near_row, place(j * sigma)).start()
        here = jnp.logical_and(own_half, k == 0)

        @pl.when(here)
        def _():
            pltpu.make_async_copy(
                u_out.at[m, pl.ds(pl.multiple_of(near_row * rows, rows), rows)],
                u_in.at[slot],
                u_recv_sem,
            ).start()

        @pl.when(jnp.logical_not(here))
        def _():
            u_copy(near_row, m).start()

        return carry

    lax.fori_loop(0, per_half // 4, send_u, 0)
    relay_copy.wait_recv()

    def pass_on(k, carry):
        near_row = (d + 7 * k) % per_half
        pltpu.make_async_remote_copy(
            src_ref=relay.at[pl.ds(pl.multiple_of(near_row * rows, rows), rows)],
            dst_ref=u_in.at[slot],
            send_sem=u_send_sem,
            recv_sem=u_recv_sem,
            device_id=((1 - h) * per_half + near_row, (partner + nm // 2) % nm),
            device_id_type=MESH,
        ).start()
        return carry

    lax.fori_loop(0, per_half, pass_on, 0)
    lax.fori_loop(per_half // 4, per_half // 2, send_u, 0)

    some_mp = sq_mp.at[pl.ds(0, nm - 1)]
    pltpu.make_async_copy(some_mp, some_mp, sq_recv_sem.at[1]).wait()
    total_sq = everything(jnp.sum(sq_mp[...], axis=0))
    clip = jnp.minimum(1.0, clip_rms * jnp.sqrt(F32(blocks * width * width)) / jnp.sqrt(total_sq + 1e-06))
    coefficient = (1.0 - beta_two) * clip * clip
    pltpu.make_async_copy(some_mp, some_mp, sum_recv_sem.at[0]).wait()
    mine = jnp.zeros((8, 128), F32)
    for p in range(pairs):
        u_total = sums[2 * p, 0:1] + sums[2 * p + 1, 0:1]
        scale = -(clip * jnp.sqrt(sums[2 * p, 4:5]) / jnp.sqrt(u_total + 1e-06))
        mine = jnp.where(row == p, scale, mine)
    scales[d] = mine

    def send_scales(k, carry):
        pltpu.make_async_remote_copy(
            src_ref=scales.at[d],
            dst_ref=scales.at[d],
            send_sem=sum_send_sem.at[1],
            recv_sem=sum_recv_sem.at[1],
            device_id=((d + k) % nd, m),
            device_id_type=MESH,
        ).start()
        return carry

    lax.fori_loop(1, nd, send_scales, 0)
    lax.fori_loop(per_half // 2, per_half, send_u, 0)

    for k in range(nm):
        full[:, k * cols : (k + 1) * cols] = slabs[k]
    loads[2].wait()

    def left_gram(n, carry):
        part = pl.ds(pl.multiple_of(n * step, step), step)
        gram = lax.dot_general(
            full[my_rows], full[part], (((1,), (1,)), ((), ())), preferred_element_type=F32
        )
        new_left[0, :, part] = beta_two * new_left[0, :, part] + coefficient * gram
        return carry

    lax.fori_loop(0, width // step, left_gram, 0)
    loads[3].wait()

    def right_gram(n, carry):
        part = pl.ds(pl.multiple_of(n * step, step), step)
        gram = lax.dot_general(
            full[:, my_rows], full[:, part], (((0,), (0,)), ((), ())), preferred_element_type=F32
        )
        new_right[0, :, part] = beta_two * new_right[0, :, part] + coefficient * gram
        return carry

    lax.fori_loop(0, width // step, right_gram, 0)

    sent = tiles.at[pl.ds(0, blocks - 1)]
    pltpu.make_async_copy(sent, sent, tile_sem).wait()
    pltpu.make_async_copy(lroot, lroot, root_sem.at[0]).wait()
    pltpu.make_async_copy(some, some, sq_send_sem.at[0]).wait()
    pltpu.make_async_copy(some_mp, some_mp, sq_send_sem.at[1]).wait()
    pltpu.make_async_copy(some_mp, some_mp, sum_send_sem.at[0]).wait()
    pltpu.make_async_copy(some, some, sum_send_sem.at[1]).wait()
    relay_copy.wait_send()
    pltpu.make_async_copy(lroot, lroot, forward_sem).wait()

    @pl.when(own_half)
    def _():
        pltpu.make_async_copy(sent, sent, u_send_sem).wait()

    @pl.when(jnp.logical_not(own_half))
    def _():
        pltpu.make_async_copy(tiles, tiles, u_send_sem).wait()

    pltpu.make_async_copy(some, some, sum_recv_sem.at[1]).wait()
    pltpu.make_async_copy(u_in, u_in, u_recv_sem).wait()


def finish_kernel(
    left, right, tiles, scales, inverse_in, new_left, new_right, update, inverse, scaled, arranged, sem
):
    places = scales.shape[0]
    blocks = tiles.shape[0]
    pairs = blocks // places
    inverse_copy = pltpu.make_async_copy(inverse_in.at[0], inverse, sem.at[0])
    inverse_copy.start()
    stores = [
        pltpu.make_async_copy(left, new_left, sem.at[1]),
        pltpu.make_async_copy(right, new_right, sem.at[2]),
    ]
    for store in stores:
        store.start()

    def scale(there, carry):
        for p in range(pairs):
            s = pairs * there + p
            scaled[s] = (tiles[s].astype(F32) * scales[there, p : p + 1]).astype(BF16)
        return carry

    lax.fori_loop(0, places, scale, 0, unroll=2)
    inverse_copy.wait()

    def give(b, carry):
        arranged[b] = scaled[inverse[b]]
        return carry

    parts = 4
    size = blocks // parts
    for n in range(parts):
        lax.fori_loop(n * size, (n + 1) * size, give, 0, unroll=min(8, size))
        part = pl.ds(n * size, size)
        stores.append(pltpu.make_async_copy(arranged.at[part], update.at[part], sem.at[3 + n]))
        stores[-1].start()
    for store in stores:
        store.wait()


def body(nd, nm, grads, order, left_stat, right_stat, left_root, right_root):
    blocks, rows, cols = grads.shape
    _, half, width = left_stat.shape
    vmem = pl.BlockSpec(memory_space=pltpu.VMEM)
    half_shape = left_stat.shape
    hbm = pl.BlockSpec(memory_space=pltpu.HBM)
    dma = pltpu.SemaphoreType.DMA
    operands = [order.reshape(1, blocks), grads, left_stat, right_stat, left_root, right_root]
    operands = [pltpu.with_memory_space_constraint(x, pltpu.HBM) for x in operands]
    products = 4 * half * width * width
    results = pl.pallas_call(
        functools.partial(kernel, nd, nm),
        out_shape=(
            pltpu.VMEM(left_stat.shape, F32),
            pltpu.VMEM(right_stat.shape, F32),
            pltpu.VMEM(grads.shape, BF16),
            pltpu.VMEM((nd, 8, 128), F32),
            pltpu.VMEM((1, blocks), jnp.int32),
        ),
        in_specs=[hbm] * 6,
        out_specs=(vmem,) * 5,
        scratch_shapes=[
            pltpu.SMEM((blocks,), jnp.int32),
            pltpu.VMEM((1, blocks), jnp.int32),
            pltpu.VMEM((blocks, rows, cols), BF16),
            pltpu.VMEM((blocks, rows, cols), BF16),
            pltpu.VMEM((nm, width, cols), BF16),
            pltpu.VMEM((width, width), BF16),
            pltpu.VMEM((half, width), BF16),
            pltpu.VMEM((width, width), BF16),
            pltpu.VMEM((half, width), F32),
            pltpu.VMEM((half, cols), BF16),
            pltpu.VMEM((nm, half, cols), BF16),
            pltpu.VMEM((half, cols), BF16),
            pltpu.VMEM((nd, 8, 128), F32),
            pltpu.VMEM((8, 128), F32),
            pltpu.VMEM((nm, 8, 128), F32),
            pltpu.VMEM((8, 128), F32),
            pltpu.VMEM((nm, 8, 128), F32),
            dma((7,)),
            dma((nm, 4)),
            dma,
            dma,
            dma((2,)),
            dma((2,)),
            dma((2,)),
            dma((2,)),
            dma((2,)),
            dma,
            dma,
            dma((2,)),
            pltpu.SemaphoreType.REGULAR,
        ],
        compiler_params=pltpu.CompilerParams(
            collective_id=0, has_side_effects=True, vmem_limit_bytes=48 * 1024 * 1024
        ),
        cost_estimate=pl.CostEstimate(
            flops=2 * products, bytes_accessed=12 * half * width * 2, transcendentals=0
        ),
        name="step",
    )(*operands)
    return pl.pallas_call(
        finish_kernel,
        out_shape=(
            pltpu.HBM(half_shape, F32),
            pltpu.HBM(half_shape, F32),
            pltpu.HBM(grads.shape, BF16),
        ),
        in_specs=[vmem] * 5,
        out_specs=(hbm, hbm, hbm),
        scratch_shapes=[
            pltpu.SMEM((blocks,), jnp.int32),
            pltpu.VMEM(grads.shape, BF16),
            pltpu.VMEM(grads.shape, BF16),
            dma((7,)),
        ],
        compiler_params=pltpu.CompilerParams(vmem_limit_bytes=8 * 1024 * 1024),
        cost_estimate=pl.CostEstimate(flops=0, bytes_accessed=10 * half * width, transcendentals=0),
        name="finish",
    )(*results)


def solution(mesh):
    owned = P(("dp", "mp"), None, None)
    return jax.shard_map(
        functools.partial(body, mesh.shape["dp"], mesh.shape["mp"]),
        mesh=mesh,
        in_specs=(P(None, "dp", "mp"), P(), owned, owned, owned, owned),
        out_specs=(owned, owned, P(None, "dp", "mp")),
        check_vma=False,
    )
```
